256 devices in a mesh: col: 8 (over x_lo, y), tok: 32 (over z, x_hi, core).
Axes of the slice: x: 4 (x_hi: 2, x_lo: 2; x = x_hi * 2 + x_lo), y: 4, z: 8, core: 2. Of those that a mesh axis runs over, the one named last changes fastest.
Arguments:
- activations: bfloat16 [32768, 8192], P('tok', 'col'), may hold values from -6 to 6
Outputs:
- factor: float32 [8192, 8192], P(('col', 'tok'))
The draws below stay inside these ranges and needn't reach their ends.
All inputs are finite; a program needn't handle non-finite values.
Results may differ from the reference program's by a relative error of at most 0.0003.
Values may be sent and summed in bfloat16 or wider, within the bound.
A program may use at most 128 MiB of HBM per device.

```python
import jax
import jax.numpy as jnp
from jax import lax

H = 8192
TOK_DEV = 1024
TOKENS = 32768
N_TOK = 32


def levels(stream_key, extent, shards, smallest, top_value):
    loudness = 1.0
    for position, blocks in shards:
        heights = jax.random.uniform(jax.random.fold_in(jax.random.fold_in(stream_key, 6), position), (blocks,), jnp.float32, smallest / len(shards), top_value / len(shards))
        loudness = loudness * jnp.repeat(jnp.exp(heights), extent[position] // blocks).reshape((-1,) + (1,) * (len(extent) - 1 - position))
    return loudness


def scatter_about(own_key, dims, scale, limit, cuts=(), dtype=jnp.bfloat16):
    entries = jax.random.normal(own_key, dims, jnp.float32) * scale
    if len(cuts) > 0:
        entries = levels(own_key, dims, cuts, -0.22, 0.18) * entries
    return jnp.clip(entries, min=-limit, max=limit).astype(dtype)


def setup_inputs(seed: int = 0) -> dict:
    streams_of = jax.random.split(jax.random.key(seed), 2)
    return {
        "activations": scatter_about(streams_of[0], (TOKENS, H), 1.0, 6.0, ((0, 32), (1, 8))),
    }


def reference(activations):
    token_blocks = activations.reshape(N_TOK, TOK_DEV, H)

    def accumulate(running_sum, token_block):
        values = token_block.astype(jnp.float32)
        product = jnp.dot(values.T, values, precision=lax.Precision.HIGHEST, preferred_element_type=jnp.float32)
        return running_sum + product, None

    start_sum = jnp.zeros((H, H), jnp.float32)
    token_sums, unused = lax.scan(accumulate, start_sum, token_blocks)
    return token_sums / jnp.float32(TOKENS)
```

```python
import jax
import jax.numpy as jnp
from jax import lax
from jax.experimental import pallas as pl
from jax.experimental.pallas import tpu as pltpu
from jax.sharding import PartitionSpec as P

MESH = pl.DeviceIdType.MESH
F32, BF16 = jnp.float32, jnp.bfloat16
BLOCK = 1024
HALF = BLOCK // 2
ROWS = 32
W = 192
LAST = (((1,), (1,)), ((), ()))
C_NEXT_OWN, C_SELF_OWN, C_NEXT_OTHER, C_OPPOSITE, C_SELF_OTHER = range(5)
CELL_REL = (1, 0, 1, 2, 0)
MIRRORED = (C_NEXT_OWN, C_NEXT_OTHER, C_OPPOSITE)


def kernel(scale, a_ref, out_ref, G, Q, RL, T, CR, ZR, R, O1, O2, MB, MT, MO,
           xs, xr, ys, yr, cs, cr, zs, zr, ds, dr, ms, mr, ts, tr):
    col, tok = lax.axis_index("col"), lax.axis_index("tok")
    lo, y = col // 4, col % 4
    z, hi, c = tok // 4, (tok // 2) % 2, tok % 2
    x = 2 * hi + lo
    s = y // 2

    def at(x_, y_, z_, c_):
        return ((x_ % 2) * 4 + y_, z_ * 4 + (x_ // 2) * 2 + c_)

    x_next, x_prev = (x + 1) % 4, (x + 3) % 4
    y_next, y_prev, y_far = (y + 1) % 4, (y + 3) % 4, (y + 2) % 4
    x_dev = (at(x_next, y, z, c), at(x_prev, y, z, c))
    y_up, y_down = at(x, y_next, z, c), at(x, y_prev, z, c)
    sibling = at(x, y, z, 1 - c)
    z_dev = (at(x, y, (z + 1) % 8, c), at(x, y, (z + 7) % 8, c))
    pending = []

    def send(src, dst, s_sem, r_sem, dev):
        cp = pltpu.make_async_remote_copy(src_ref=src, dst_ref=dst, send_sem=s_sem, recv_sem=r_sem,
                                          device_id=dev, device_id_type=MESH)
        cp.start()
        pending.append(cp)
        return cp

    def arrived(dst, s_sem, r_sem):
        pltpu.make_async_remote_copy(src_ref=dst, dst_ref=dst, send_sem=s_sem, recv_sem=r_sem,
                                     device_id=sibling, device_id_type=MESH).wait_recv()

    partners = [at(2 * (hi ^ dh) + (lo ^ dl), y, z, c ^ dc)
                for dh in range(2) for dl in range(2) for dc in range(2) if dh + dl + dc]
    partners += [at(x, y, (z + dz) % 8, c) for dz in range(1, 8)]
    partners += [at(x, (y + dy) % 4, z, c) for dy in range(1, 4)]
    barrier = pltpu.get_barrier_semaphore()
    for dev in partners:
        pl.semaphore_signal(barrier, inc=1, device_id=dev, device_id_type=MESH)
    pl.semaphore_wait(barrier, len(partners))

    def reorder(h, part):
        p = lax.broadcasted_iota(jnp.int32, (BLOCK, HALF), 1)
        f = lax.broadcasted_iota(jnp.int32, (BLOCK, HALF), 0)
        feature = ((p // 32) % 8) * 128 + h * 64 + (p // 256) * 32 + p % 32
        pick = (f == feature).astype(F32).astype(BF16)
        rows = pl.ds(part * HALF, HALF)
        G[x, h, rows, :] = jnp.dot(a_ref[rows, :], pick, preferred_element_type=F32).astype(BF16)

    def turn(x_from, slot):
        r = lax.broadcasted_iota(jnp.int32, (HALF, HALF), 0)
        f = lax.broadcasted_iota(jnp.int32, (HALF, HALF), 1)
        one = (r == f).astype(F32).astype(BF16)
        Q[0, slot] = lax.dot_general(one, G[x_from, hi], LAST, preferred_element_type=F32).astype(BF16)

    def x_unit(x_, h, part):
        return G.at[x_, h, pl.ds(part * HALF, HALF), :]

    def x_send(d, step, x_, h, part):
        return send(x_unit(x_, h, part), x_unit(x_, h, part), xs.at[d, step], xr.at[d, step], x_dev[d])

    x_from = (x_prev, x_next)

    def x_arrived(d, step, h, part):
        arrived(x_unit(x_from[d], h, part), xs.at[d, step], xr.at[d, step])

    def h_of(x_):
        return x_ // 2

    def y_sends(k, slot):
        low, high = pl.ds(0, W), pl.ds(W, HALF - W)
        send(Q.at[0, slot, low], Q.at[1, slot, low], ys.at[k, 0], yr.at[k, 0], y_down)
        send(Q.at[0, slot, high], RL.at[k], ys.at[k, 2], yr.at[k, 2], y_up)
        send(Q.at[0, slot, high], Q.at[1, slot, high], ys.at[k, 1], yr.at[k, 1], y_down)

    def y_forward(k, slot):
        low, high = pl.ds(0, W), pl.ds(W, HALF - W)
        arrived(Q.at[1, slot, low], ys.at[k, 0], yr.at[k, 0])
        send(Q.at[1, slot, low], Q.at[2, slot, low], ys.at[k, 3], yr.at[k, 3], y_down)
        arrived(RL.at[k], ys.at[k, 2], yr.at[k, 2])
        send(RL.at[k], Q.at[2, slot, high], ys.at[k, 4], yr.at[k, 4], y_up)

    cell_lo = (lo, lo, 1 - lo, (lo + s) % 2, 1 - lo)

    def compute(cell):
        rel, l = CELL_REL[cell], cell_lo[cell]

        @pl.loop(0, 4)
        def _(n):
            h, cols = n // 2, pl.ds(pl.multiple_of((n % 2) * 256, 256), 256)
            acc = jnp.dot(Q[rel, 0], G[l, h, :, cols], preferred_element_type=F32)
            acc += jnp.dot(Q[rel, 1], G[2 + l, h, :, cols], preferred_element_type=F32)
            T[cell, :, :, :, pl.ds(pl.multiple_of(n * 256, 256), 256)] = acc.reshape(2, 8, ROWS, 256)

        send(T.at[cell, 1 - c], CR.at[cell], cs.at[cell], cr.at[cell], sibling)

    def core_arrived(cell):
        arrived(CR.at[cell], cs.at[cell], cr.at[cell])

    sides = (pl.ds(0, HALF), pl.ds(HALF, HALF))

    def z_landed(cell, d, step):
        part = ZR.at[cell, d, 0, :, sides[d]] if step == 0 else ZR.at[cell, d, step]
        arrived(part, zs.at[cell, d, step], zr.at[cell, d, step])

    def z_step(cell, step):
        for d in range(2):
            to = (z + 4 - step) % 8 if d == 0 else (z + 4 + step) % 8
            if step > 0:
                z_landed(cell, d, step - 1)
            if step == 0:
                cols = sides[d]
                T[cell, c, to, :, cols] = T[cell, c, to, :, cols] + CR[cell, to, :, cols]
                send(T.at[cell, c, to, :, cols], ZR.at[cell, d, 0, :, cols], zs.at[cell, d, 0], zr.at[cell, d, 0], z_dev[d])
                continue
            if step == 1:
                cols, rest = sides[d], sides[1 - d]
                T[cell, c, to, :, cols] = T[cell, c, to, :, cols] + CR[cell, to, :, cols] + ZR[cell, d, 0, :, cols]
                T[cell, c, to, :, rest] = T[cell, c, to, :, rest] + CR[cell, to, :, rest]
            else:
                T[cell, c, to] = T[cell, c, to] + CR[cell, to] + ZR[cell, d, step - 1]
            send(T.at[cell, c, to], ZR.at[cell, d, step], zs.at[cell, d, step], zr.at[cell, d, step], z_dev[d])

    def total(cell):
        z_landed(cell, 0, 3)
        z_landed(cell, 1, 3)
        return (T[cell, c, z] + CR[cell, z] + ZR[cell, 0, 3] + ZR[cell, 1, 3]) * scale

    def natural(v):
        return jnp.concatenate([v[:, h * HALF + k * 256 + b * 32:h * HALF + k * 256 + b * 32 + 32]
                                for b in range(8) for h in range(2) for k in range(2)], axis=1)

    def out_cols(l, y_):
        return pl.ds(pl.multiple_of((l * 4 + y_) * BLOCK, BLOCK), BLOCK)

    def group(h, k):
        return pl.ds(pl.multiple_of(h * HALF + k * 256, 256), 256)

    def mirror_slot(m, h, k, l):
        return (8 if m == 2 else l * 4) + h * 2 + k

    def spread(m):
        cell = MIRRORED[m]
        R[m] = total(cell)
        if m == 2:
            send(R.at[m], O2, ds.at[m], dr.at[m], at(x, y_far, z, c))
        else:
            send(R.at[m], O1.at[cell_lo[cell]], ds.at[m], dr.at[m], y_up)
        mine = mirror_slot(m, hi, c, lo)
        for dh in range(2):
            for dc in range(2):
                h, k = (hi + dh) % 2, (c + dc) % 2
                src = R.at[m, :, group(h, k)]
                dev = at(2 * h + cell_lo[cell], y, z, k)
                if dh + dc or m == 1:
                    send(src, MB.at[mine], ms.at[m, dh, dc], mr.at[m, dh, dc], dev)
                elif m == 0:
                    MB[mine] = R[m, :, group(h, k)]
                else:
                    @pl.when(s == 0)
                    def _():
                        MB[mine] = R[m, :, group(h, k)]

                    @pl.when(s == 1)
                    def _():
                        pltpu.make_async_remote_copy(
                            src_ref=src, dst_ref=MB.at[mine], send_sem=ms.at[m, dh, dc], recv_sem=mr.at[m, dh, dc],
                            device_id=dev, device_id_type=MESH).start()

    def spread_arrived():
        for m in range(3):
            l = (lo, 1 - lo, (lo + s) % 2)[m]
            for dh in range(2):
                for dc in range(2):
                    slot = mirror_slot(m, (hi + dh) % 2, (c + dc) % 2, l)
                    if dh + dc or m == 1:
                        arrived(MB.at[slot], ms.at[m, dh, dc], mr.at[m, dh, dc])
                    elif m == 2:
                        @pl.when(s == 1)
                        def _():
                            cp = pltpu.make_async_remote_copy(
                                src_ref=MB.at[slot], dst_ref=MB.at[slot], send_sem=ms.at[m, dh, dc],
                                recv_sem=mr.at[m, dh, dc], device_id=sibling, device_id_type=MESH)
                            cp.wait_recv()
                            cp.wait_send()

    for part in range(2):
        reorder(1 - hi, part)
        x_send(part, 0, x, 1 - hi, part)
    for part in range(2):
        reorder(hi, part)
    turn(x, hi)
    y_sends(0, hi)
    for d in range(2):
        x_arrived(d, 0, 1 - h_of(x_from[d]), d)
        x_send(d, 1, x_from[d], 1 - h_of(x_from[d]), d)
    y_forward(0, hi)
    x_opposite = (x + 2) % 4
    for d in range(2):
        arrived(x_unit(x_opposite, hi, d), xs.at[d, 1], xr.at[d, 1])
        x_send(d, 2, x, hi, d)
    turn(x_opposite, 1 - hi)
    y_sends(1, 1 - hi)
    for d in range(2):
        x_arrived(d, 2, h_of(x_from[d]), d)
        x_send(d, 3, x_from[d], h_of(x_from[d]), d)
    y_forward(1, 1 - hi)
    for d in range(2):
        arrived(x_unit(x_opposite, 1 - hi, d), xs.at[d, 3], xr.at[d, 3])
        x_send(d, 4, x, 1 - hi, 1 - d)
        x_send(d, 5, x, hi, 1 - d)

    compute(C_SELF_OWN)
    core_arrived(C_SELF_OWN)
    z_step(C_SELF_OWN, 0)
    high = pl.ds(W, HALF - W)
    for k, slot in ((0, hi), (1, 1 - hi)):
        arrived(Q.at[1, slot, high], ys.at[k, 1], yr.at[k, 1])
    compute(C_NEXT_OWN)
    z_step(C_SELF_OWN, 1)
    core_arrived(C_NEXT_OWN)
    z_step(C_NEXT_OWN, 0)
    z_step(C_SELF_OWN, 2)
    z_step(C_NEXT_OWN, 1)
    z_step(C_SELF_OWN, 3)
    z_step(C_NEXT_OWN, 2)
    for d in range(2):
        x_arrived(d, 4, 1 - h_of(x_from[d]), 1 - d)
        x_arrived(d, 5, h_of(x_from[d]), 1 - d)
    compute(C_NEXT_OTHER)
    z_step(C_NEXT_OWN, 3)
    for k, slot in ((0, hi), (1, 1 - hi)):
        arrived(Q.at[2, slot, pl.ds(0, W)], ys.at[k, 3], yr.at[k, 3])
        arrived(Q.at[2, slot, high], ys.at[k, 4], yr.at[k, 4])
    core_arrived(C_NEXT_OTHER)
    z_step(C_NEXT_OTHER, 0)
    compute(C_OPPOSITE)
    spread(0)
    z_step(C_NEXT_OTHER, 1)
    core_arrived(C_OPPOSITE)
    z_step(C_OPPOSITE, 0)
    compute(C_SELF_OTHER)
    z_step(C_NEXT_OTHER, 2)
    z_step(C_OPPOSITE, 1)
    core_arrived(C_SELF_OTHER)
    z_step(C_SELF_OTHER, 0)
    z_step(C_NEXT_OTHER, 3)
    z_step(C_OPPOSITE, 2)
    z_step(C_SELF_OTHER, 1)
    spread(1)
    z_step(C_OPPOSITE, 3)
    z_step(C_SELF_OTHER, 2)
    spread(2)
    z_step(C_SELF_OTHER, 3)
    spread_arrived()
    turned = jnp.transpose(MB[...].reshape(12 * ROWS, 256)).reshape(8, ROWS, 12 * ROWS)
    MT[...] = turned
    MO[z] = MT[z]
    for dz in range(1, 8):
        to = (z + dz) % 8
        send(MT.at[to], MO.at[z], ts.at[dz], tr.at[dz], at(x, y, to, c))
    out_ref[:, out_cols(lo, y)] = natural(total(C_SELF_OWN))
    out_ref[:, out_cols(1 - lo, y)] = natural(total(C_SELF_OTHER))
    for m, l in ((0, lo), (1, 1 - lo)):
        arrived(O1.at[l], ds.at[m], dr.at[m])
        out_ref[:, out_cols(l, y_prev)] = natural(O1[l])
    arrived(O2, ds.at[2], dr.at[2])
    out_ref[:, out_cols((lo + 1 - s) % 2, y_far)] = natural(O2[...])
    for dz in range(1, 8):
        arrived(MO.at[(z + 8 - dz) % 8], ts.at[dz], tr.at[dz])
    for l in range(2):
        out_ref[:, out_cols(l, y_next)] = jnp.concatenate([MO[b, :, l * 128:l * 128 + 128] for b in range(8)], axis=1)
    out_ref[:, out_cols((lo + s) % 2, y_far)] = jnp.concatenate([MO[b, :, 256:384] for b in range(8)], axis=1)
    for cp in pending:
        cp.wait_send()


def solution(mesh):
    token_ranks = mesh.shape["tok"]

    def shards(activations):
        scale = 1.0 / (activations.shape[0] * token_ranks)
        dma = pltpu.SemaphoreType.DMA
        return pl.pallas_call(
            lambda *refs: kernel(scale, *refs),
            out_shape=jax.ShapeDtypeStruct((ROWS, 8 * BLOCK), F32),
            in_specs=[pl.BlockSpec(memory_space=pltpu.VMEM)],
            out_specs=pl.BlockSpec(memory_space=pltpu.VMEM),
            scratch_shapes=[
                pltpu.VMEM((4, 2, BLOCK, HALF), BF16),
                pltpu.VMEM((3, 2, HALF, BLOCK), BF16),
                pltpu.VMEM((2, HALF - W, BLOCK), BF16),
                pltpu.VMEM((5, 2, 8, ROWS, BLOCK), F32),
                pltpu.VMEM((5, 8, ROWS, BLOCK), F32),
                pltpu.VMEM((5, 2, 4, ROWS, BLOCK), F32),
                pltpu.VMEM((3, ROWS, BLOCK), F32),
                pltpu.VMEM((2, ROWS, BLOCK), F32),
                pltpu.VMEM((ROWS, BLOCK), F32),
                pltpu.VMEM((12, ROWS, 256), F32),
                pltpu.VMEM((8, ROWS, 12 * ROWS), F32),
                pltpu.VMEM((8, ROWS, 12 * ROWS), F32),
                dma((2, 6)), dma((2, 6)),
                dma((2, 5)), dma((2, 5)),
                dma((5,)), dma((5,)),
                dma((5, 2, 4)), dma((5, 2, 4)),
                dma((3,)), dma((3,)),
                dma((3, 2, 2)), dma((3, 2, 2)),
                dma((8,)), dma((8,)),
            ],
            compiler_params=pltpu.CompilerParams(
                collective_id=0, has_side_effects=True, vmem_limit_bytes=56 * 1024 * 1024),
            cost_estimate=pl.CostEstimate(flops=14 * 10**9, bytes_accessed=3 * 2**20, transcendentals=0),
            name="gram",
        )(activations)

    return jax.shard_map(shards, mesh=mesh, in_specs=(P("tok", "col"),), out_specs=P(("col", "tok"), None), check_vma=False)
```

```python
import jax
import jax.numpy as jnp
from jax import lax
from jax.experimental import pallas as pl
from jax.experimental.pallas import tpu as pltpu
from jax.sharding import PartitionSpec as P

MESH = pl.DeviceIdType.MESH
F32, BF16 = jnp.float32, jnp.bfloat16
BLOCK = 1024
HALF = BLOCK // 2
ROWS = 32
W = 160
LAST = (((1,), (1,)), ((), ()))
CELLS = 12
OWN = (0, 1, 2, 3)
CELL_REL = (0, 0, None, None, 0, 1, 1, 1, 1, 2, 2, 0)
TO_NEXT = (5, 6, 7, 8)
TO_FAR = (9, 10)


def kernel(scale, a_ref, out_ref, G, Q, QP, RL, T, CR, ZR, R, PR, O1, O2, MB, MT, MO, OUT,
           xs, xr, ys, yr, cs, cr, zs, zr, ds, dr, ms, mr, ts, tr, os):
    col, tok = lax.axis_index("col"), lax.axis_index("tok")
    lo, y = col // 4, col % 4
    z, hi, c = tok // 4, (tok // 2) % 2, tok % 2
    x = 2 * hi + lo
    s = y // 2

    def at(x_, y_, z_, c_):
        return ((x_ % 2) * 4 + y_, z_ * 4 + (x_ // 2) * 2 + c_)

    x_next, x_prev = (x + 1) % 4, (x + 3) % 4
    y_next, y_prev, y_far = (y + 1) % 4, (y + 3) % 4, (y + 2) % 4
    x_dev = (at(x_next, y, z, c), at(x_prev, y, z, c))
    y_up, y_down = at(x, y_next, z, c), at(x, y_prev, z, c)
    sibling = at(x, y, z, 1 - c)
    z_dev = (at(x, y, (z + 1) % 8, c), at(x, y, (z + 7) % 8, c))
    pending = []

    def send(src, dst, s_sem, r_sem, dev):
        cp = pltpu.make_async_remote_copy(src_ref=src, dst_ref=dst, send_sem=s_sem, recv_sem=r_sem,
                                          device_id=dev, device_id_type=MESH)
        cp.start()
        pending.append(cp)
        return cp

    def arrived(dst, s_sem, r_sem):
        pltpu.make_async_remote_copy(src_ref=dst, dst_ref=dst, send_sem=s_sem, recv_sem=r_sem,
                                     device_id=sibling, device_id_type=MESH).wait_recv()

    partners = [at(2 * (hi ^ dh) + (lo ^ dl), y, z, c ^ dc)
                for dh in range(2) for dl in range(2) for dc in range(2) if dh + dl + dc]
    partners += [at(x, y, (z + dz) % 8, c) for dz in range(1, 8)]
    partners += [at(x, (y + dy) % 4, z, c) for dy in range(1, 4)]
    barrier = pltpu.get_barrier_semaphore()
    for dev in partners:
        pl.semaphore_signal(barrier, inc=1, device_id=dev, device_id_type=MESH)

    def reorder(h, part):
        p = lax.broadcasted_iota(jnp.int32, (BLOCK, HALF), 1)
        f = lax.broadcasted_iota(jnp.int32, (BLOCK, HALF), 0)
        feature = ((p // 32) % 8) * 128 + h * 64 + (p // 256) * 32 + p % 32
        pick = (f == feature).astype(F32).astype(BF16)
        rows = pl.ds(part * HALF, HALF)
        G[x, h, rows, :] = jnp.dot(a_ref[rows, :], pick, preferred_element_type=F32).astype(BF16)

    def turn(x_from, h, dst):
        r = lax.broadcasted_iota(jnp.int32, (HALF, HALF), 0)
        f = lax.broadcasted_iota(jnp.int32, (HALF, HALF), 1)
        one = (r == f).astype(F32).astype(BF16)
        dst[...] = lax.dot_general(one, G[x_from, h], LAST, preferred_element_type=F32).astype(BF16)

    def x_unit(x_, h, part):
        return G.at[x_, h, pl.ds(part * HALF, HALF), :]

    def x_send(d, step, x_, h, part):
        return send(x_unit(x_, h, part), x_unit(x_, h, part), xs.at[d, step], xr.at[d, step], x_dev[d])

    x_from = (x_prev, x_next)

    def x_arrived(d, step, h, part):
        arrived(x_unit(x_from[d], h, part), xs.at[d, step], xr.at[d, step])

    def h_of(x_):
        return x_ // 2

    low, high = pl.ds(0, W), pl.ds(W, HALF - W)

    def y_sends(k, slot):
        send(Q.at[0, slot, low], Q.at[1, slot, low], ys.at[k, 0], yr.at[k, 0], y_down)
        send(Q.at[0, slot, high], RL.at[k], ys.at[k, 2], yr.at[k, 2], y_up)
        send(Q.at[0, slot, high], Q.at[1, slot, high], ys.at[k, 1], yr.at[k, 1], y_down)

    def y_forward_down(k, slot):
        arrived(Q.at[1, slot, low], ys.at[k, 0], yr.at[k, 0])
        send(Q.at[1, slot, low], Q.at[2, slot, low], ys.at[k, 3], yr.at[k, 3], y_down)

    def y_forward_up(k, slot):
        arrived(RL.at[k], ys.at[k, 2], yr.at[k, 2])
        send(RL.at[k], Q.at[2, slot, high], ys.at[k, 4], yr.at[k, 4], y_up)

    slots = ((0, hi), (1, 1 - hi))
    far_lo = (lo + s) % 2
    cell_lo = (lo, lo, lo, lo, 1 - lo, lo, 1 - lo, 1 - lo, lo, far_lo, far_lo, 1 - lo)
    cell_h = (hi, 1 - hi, hi, 1 - hi, 0, hi, 0, 1, 1 - hi, hi, 1 - hi, 1)

    def compute(cell):
        rel, l, h = CELL_REL[cell], cell_lo[cell], cell_h[cell]

        @pl.loop(0, 2)
        def _(n):
            cols = pl.ds(pl.multiple_of(n * 256, 256), 256)
            if cell in OWN:
                rows = QP[...] if rel is None else Q[rel, hi]
                acc = jnp.dot(rows, G[x, h, :, cols], preferred_element_type=F32)
            else:
                acc = jnp.dot(Q[rel, 0], G[l, h, :, cols], preferred_element_type=F32)
                acc += jnp.dot(Q[rel, 1], G[2 + l, h, :, cols], preferred_element_type=F32)
            T[cell, :, :, :, cols] = acc.reshape(2, 8, ROWS, 256)

        send(T.at[cell, 1 - c], CR.at[cell], cs.at[cell], cr.at[cell], sibling)

    sides = (pl.ds(0, 256), pl.ds(256, 256))

    def z_landed(cell, d, step):
        part = ZR.at[cell, d, 0, :, sides[d]] if step == 0 else ZR.at[cell, d, step]
        arrived(part, zs.at[cell, d, step], zr.at[cell, d, step])

    def z_step(cell, step):
        if step == 0:
            arrived(CR.at[cell], cs.at[cell], cr.at[cell])
        for d in range(2):
            to = (z + 4 - step) % 8 if d == 0 else (z + 4 + step) % 8
            if step > 0:
                z_landed(cell, d, step - 1)
            if step == 0:
                cols = sides[d]
                T[cell, c, to, :, cols] = T[cell, c, to, :, cols] + CR[cell, to, :, cols]
                send(T.at[cell, c, to, :, cols], ZR.at[cell, d, 0, :, cols], zs.at[cell, d, 0], zr.at[cell, d, 0], z_dev[d])
                continue
            if step == 1:
                cols, rest = sides[d], sides[1 - d]
                T[cell, c, to, :, cols] = T[cell, c, to, :, cols] + CR[cell, to, :, cols] + ZR[cell, d, 0, :, cols]
                T[cell, c, to, :, rest] = T[cell, c, to, :, rest] + CR[cell, to, :, rest]
            else:
                T[cell, c, to] = T[cell, c, to] + CR[cell, to] + ZR[cell, d, step - 1]
            send(T.at[cell, c, to], ZR.at[cell, d, step], zs.at[cell, d, step], zr.at[cell, d, step], z_dev[d])

    def total(cell):
        z_landed(cell, 0, 3)
        z_landed(cell, 1, 3)
        return T[cell, c, z] + CR[cell, z] + ZR[cell, 0, 3] + ZR[cell, 1, 3]

    def natural(v):
        return scale * jnp.concatenate([v[h][:, k * 256 + b * 32:k * 256 + b * 32 + 32]
                                        for b in range(8) for h in range(2) for k in range(2)], axis=1)

    def out_cols(l, y_):
        return pl.ds(pl.multiple_of((l * 4 + y_) * BLOCK, BLOCK), BLOCK)

    def group(k):
        return pl.ds(pl.multiple_of(k * 256, 256), 256)

    mine_next, mine_far = lo * 4 + hi * 2 + c, 8 + hi * 2 + c

    def spread(cell):
        l, h = cell_lo[cell], cell_h[cell]
        R[cell] = total(cell)
        if cell in TO_FAR:
            send(R.at[cell], O2.at[h], ds.at[cell], dr.at[cell], at(x, y_far, z, c))
        else:
            send(R.at[cell], O1.at[l, h], ds.at[cell], dr.at[cell], y_up)
        mine = mine_far if cell in TO_FAR else mine_next
        for dk in range(2):
            k = (c + dk) % 2
            src, dev = R.at[cell, :, group(k)], at(2 * h + l, y, z, k)
            if dk or cell not in (5, 9):
                send(src, MB.at[mine], ms.at[cell, dk], mr.at[mine], dev)
            elif cell == 5:
                MB[mine] = R[cell, :, group(k)]
            else:
                @pl.when(s == 0)
                def _():
                    MB[mine] = R[cell, :, group(k)]

                @pl.when(s == 1)
                def _():
                    pltpu.make_async_remote_copy(
                        src_ref=src, dst_ref=MB.at[mine], send_sem=ms.at[cell, dk], recv_sem=mr.at[mine],
                        device_id=dev, device_id_type=MESH).start()

    def swap_own():
        for cell in (2, 3):
            R[cell] = total(cell)
            send(R.at[cell], PR.at[cell_h[cell]], ds.at[cell], dr.at[cell], at(x_opposite, y, z, c))

    mirror_base = ((1 - lo) * 4, lo * 4, 8)

    def mirror(b):
        for n in range(4):
            slot = mirror_base[b] + n
            if b == 0:
                arrived(MB.at[slot], ms.at[5, 0], mr.at[slot])
            else:
                @pl.when((n != hi * 2 + c) | ((s == 1) if b == 2 else False))
                def _():
                    arrived(MB.at[slot], ms.at[5, 0], mr.at[slot])
        if b == 2:
            @pl.when(s == 1)
            def _():
                pltpu.make_async_remote_copy(
                    src_ref=R.at[9, :, group(c)], dst_ref=MB.at[mine_far], send_sem=ms.at[9, 0], recv_sem=mr.at[mine_far],
                    device_id=sibling, device_id_type=MESH).wait_send()
        MT[b] = jnp.transpose(MB[pl.ds(mirror_base[b], 4)].reshape(4 * ROWS, 256)).reshape(8, ROWS, 4 * ROWS) * scale
        MO[b, z] = MT[b, z]
        for dz in range(1, 8):
            to = (z + dz) % 8
            send(MT.at[b, to], MO.at[b, z], ts.at[b, dz], tr.at[b, dz], at(x, y, to, c))

    stored = []

    def store(n, l, y_, v):
        OUT[n] = v
        cp = pltpu.make_async_copy(OUT.at[n], out_ref.at[:, out_cols(l, y_)], os.at[n])
        cp.start()
        stored.append(cp)

    def store_mirror(b, l, y_):
        for dz in range(1, 8):
            arrived(MO.at[b, (z + 8 - dz) % 8], ts.at[b, dz], tr.at[b, dz])
        store(5 + b, l, y_, jnp.concatenate([MO[b, k] for k in range(8)], axis=1))

    x_opposite = (x + 2) % 4
    for part in range(2):
        reorder(1 - hi, part)
    pl.semaphore_wait(barrier, len(partners))
    for part in range(2):
        x_send(part, 0, x, 1 - hi, part)
    for part in range(2):
        reorder(hi, part)
    turn(x, hi, Q.at[0, hi])
    y_sends(0, hi)
    compute(0)
    compute(1)
    z_step(0, 0)
    turn(x, 1 - hi, QP)
    compute(2)
    z_step(1, 0)
    z_step(0, 1)
    compute(3)
    z_step(2, 0)
    z_step(1, 1)
    z_step(0, 2)
    for d in range(2):
        x_arrived(d, 0, 1 - h_of(x_from[d]), d)
        x_send(d, 1, x_from[d], 1 - h_of(x_from[d]), d)
    z_step(3, 0)
    z_step(2, 1)
    z_step(1, 2)
    z_step(0, 3)
    y_forward_up(0, hi)
    z_step(3, 1)
    z_step(2, 2)
    z_step(1, 3)
    z_step(3, 2)
    z_step(2, 3)
    for d in range(2):
        arrived(x_unit(x_opposite, hi, d), xs.at[d, 1], xr.at[d, 1])
        x_send(d, 2, x, hi, d)
        x_send(d, 4, x, 0, 1 - d)
    turn(x_opposite, hi, Q.at[0, 1 - hi])
    y_sends(1, 1 - hi)
    z_step(3, 3)
    swap_own()
    y_forward_up(1, 1 - hi)
    for d in range(2):
        x_arrived(d, 2, h_of(x_from[d]), d)
        x_arrived(d, 4, 0, 1 - d)
        x_send(d, 5, x, 1, 1 - d)
        x_send(d, 3, x_from[d], h_of(x_from[d]), d)
    compute(4)
    for k, slot in slots:
        y_forward_down(k, slot)
        arrived(Q.at[1, slot, high], ys.at[k, 1], yr.at[k, 1])
    compute(5)
    compute(6)
    z_step(4, 0)
    z_step(5, 0)
    z_step(6, 0)
    z_step(4, 1)
    z_step(5, 1)
    z_step(6, 1)
    z_step(4, 2)
    z_step(5, 2)
    z_step(6, 2)
    z_step(4, 3)
    z_step(5, 3)
    z_step(6, 3)
    for d in range(2):
        x_arrived(d, 5, 1, 1 - d)
    for k, slot in slots:
        arrived(Q.at[2, slot, low], ys.at[k, 3], yr.at[k, 3])
        arrived(Q.at[2, slot, high], ys.at[k, 4], yr.at[k, 4])
    compute(9)
    compute(7)
    spread(5)
    spread(6)
    z_step(9, 0)
    for d in range(2):
        arrived(x_unit(x_opposite, 1 - hi, d), xs.at[d, 3], xr.at[d, 3])
    compute(8)
    compute(10)
    z_step(9, 1)
    z_step(7, 0)
    z_step(8, 0)
    z_step(10, 0)
    z_step(9, 2)
    z_step(7, 1)
    z_step(8, 1)
    z_step(10, 1)
    z_step(9, 3)
    compute(11)
    z_step(7, 2)
    z_step(8, 2)
    z_step(11, 0)
    z_step(10, 2)
    spread(9)
    z_step(7, 3)
    z_step(8, 3)
    z_step(11, 1)
    z_step(10, 3)
    spread(7)
    spread(8)
    mirror(0)
    z_step(11, 2)
    mirror(1)
    spread(10)
    mirror(2)
    z_step(11, 3)
    for cell in (2, 3):
        arrived(PR.at[1 - cell_h[cell]], ds.at[cell], dr.at[cell])
    first, second = total(0) + PR[hi], total(1) + PR[1 - hi]
    store(0, lo, y, natural((jnp.where(hi == 0, first, second), jnp.where(hi == 0, second, first))))
    for cell in TO_NEXT:
        arrived(O1.at[cell_lo[cell], cell_h[cell]], ds.at[cell], dr.at[cell])
    for l in range(2):
        store(1 + l, l, y_prev, natural(O1[l]))
    store_mirror(0, 1 - lo, y_next)
    for cell in TO_FAR:
        arrived(O2.at[cell_h[cell]], ds.at[cell], dr.at[cell])
    store(3, (lo + 1 - s) % 2, y_far, natural(O2[...]))
    store(4, 1 - lo, y, natural((total(4), total(11))))
    store_mirror(1, lo, y_next)
    store_mirror(2, far_lo, y_far)
    for cp in pending:
        cp.wait_send()
    for cp in stored:
        cp.wait()


def solution(mesh):
    token_ranks = mesh.shape["tok"]

    def shards(activations):
        scale = 1.0 / (activations.shape[0] * token_ranks)
        dma = pltpu.SemaphoreType.DMA
        return pl.pallas_call(
            lambda *refs: kernel(scale, *refs),
            out_shape=jax.ShapeDtypeStruct((ROWS, 8 * BLOCK), F32),
            in_specs=[pl.BlockSpec(memory_space=pltpu.VMEM)],
            out_specs=pl.BlockSpec(memory_space=pl.ANY),
            scratch_shapes=[
                pltpu.VMEM((4, 2, BLOCK, HALF), BF16),
                pltpu.VMEM((3, 2, HALF, BLOCK), BF16),
                pltpu.VMEM((HALF, BLOCK), BF16),
                pltpu.VMEM((2, HALF - W, BLOCK), BF16),
                pltpu.VMEM((CELLS, 2, 8, ROWS, HALF), F32),
                pltpu.VMEM((CELLS, 8, ROWS, HALF), F32),
                pltpu.VMEM((CELLS, 2, 4, ROWS, HALF), F32),
                pltpu.VMEM((CELLS, ROWS, HALF), F32),
                pltpu.VMEM((2, ROWS, HALF), F32),
                pltpu.VMEM((2, 2, ROWS, HALF), F32),
                pltpu.VMEM((2, ROWS, HALF), F32),
                pltpu.VMEM((12, ROWS, 256), F32),
                pltpu.VMEM((3, 8, ROWS, 4 * ROWS), F32),
                pltpu.VMEM((3, 8, ROWS, 4 * ROWS), F32),
                pltpu.VMEM((8, ROWS, BLOCK), F32),
                dma((2, 6)), dma((2, 6)),
                dma((2, 5)), dma((2, 5)),
                dma((CELLS,)), dma((CELLS,)),
                dma((CELLS, 2, 4)), dma((CELLS, 2, 4)),
                dma((CELLS,)), dma((CELLS,)),
                dma((CELLS, 2)), dma((12,)),
                dma((3, 8)), dma((3, 8)),
                dma((8,)),
            ],
            compiler_params=pltpu.CompilerParams(
                collective_id=0, has_side_effects=True, vmem_limit_bytes=56 * 1024 * 1024),
            cost_estimate=pl.CostEstimate(flops=14 * 10**9, bytes_accessed=3 * 2**20, transcendentals=0),
            name="gram",
        )(activations)

    return jax.shard_map(shards, mesh=mesh, in_specs=(P("tok", "col"),), out_specs=P(("col", "tok"), None), check_vma=False)
```

```python
import jax
import jax.numpy as jnp
from jax import lax
from jax.experimental import pallas as pl
from jax.experimental.pallas import tpu as pltpu
from jax.sharding import PartitionSpec as P

MESH = pl.DeviceIdType.MESH
F32, BF16 = jnp.float32, jnp.bfloat16
BLOCK = 1024
HALF = BLOCK // 2
CH = HALF // 2
ROWS = 32
PART = ROWS // 2
W = 80
LAST = (((1,), (1,)), ((), ()))
A, B = 0, 1
OWN, PEER, SELF, NEXT, FAR = range(5)
CELLS = (
    ((OWN, A, "p", A), (OWN, A, "p", B)),
    ((OWN, A, "r", A), (OWN, A, "r", B)),
    ((OWN, B, "p", A), (OWN, B, "p", B)),
    ((OWN, B, "r", A), (OWN, B, "r", B)),
    ((PEER, A, "p", A), (PEER, A, "p", B)),
    ((PEER, A, "r", A), (PEER, A, "r", B)),
    ((PEER, B, "p", A), (PEER, B, "p", B)),
    ((PEER, B, "r", A), (PEER, B, "r", B)),
    ((SELF, A, "1", A), (NEXT, A, "1", A)),
    ((NEXT, A, "r", B), (NEXT, B, "r", B)),
    ((NEXT, A, "p", B), (NEXT, A, "p", A)),
    ((SELF, A, "1", B), (SELF, B, "1", B)),
    ((SELF, A, "0", A), (SELF, B, "0", A)),
    ((SELF, B, "1", A), (NEXT, A, "0", A)),
    ((NEXT, A, "0", B), (SELF, B, "0", B)),
    ((FAR, B, "f", A), (FAR, B, "g", A)),
    ((NEXT, B, "1", A), (NEXT, B, "r", A)),
    ((NEXT, A, "r", A), (NEXT, B, "p", B)),
    ((FAR, A, "f", A), (FAR, A, "g", A)),
    ((FAR, A, "f", B), (FAR, A, "g", B)),
    ((SELF, A, "0", B), (NEXT, B, "0", B)),
    ((NEXT, A, "1", B), (NEXT, B, "1", B)),
    ((NEXT, B, "0", A), (NEXT, B, "p", A)),
    ((FAR, B, "g", B), (FAR, B, "f", B)),
)
COUNT = len(CELLS)
X_NEEDS = {("p", A): (1,), ("p", B): (3,), ("r", A): (7,), ("r", B): (11,), ("0", A): (0, 4, 5), ("0", B): (2, 8, 9),
           ("1", A): (0, 4, 6), ("1", B): (2, 8, 10), ("f", A): (1, 0, 4, 5, 6), ("f", B): (3, 2, 8, 9, 10),
           ("g", A): (7, 0, 4, 5, 6), ("g", B): (11, 2, 8, 9, 10)}
ORDER = (
    ('c', 0), ('c', 1), ('c', 2), ('c', 3), ('c', 4), ('c', 5), ('c', 6), ('z', 0, 0),
    ('z', 1, 0), ('x', 1), ('z', 2, 0), ('z', 3, 0), ('z', 4, 0), ('z', 5, 0), ('z', 6, 0), ('z', 0, 1),
    ('z', 1, 1), ('z', 2, 1), ('z', 3, 1), ('z', 4, 1), ('y', 0, 0, 4), ('z', 5, 1), ('z', 6, 1), ('z', 0, 2),
    ('z', 1, 2), ('z', 2, 2), ('x', 2), ('z', 3, 2), ('z', 4, 2), ('z', 5, 2), ('z', 6, 2), ('z', 0, 3),
    ('c', 7), ('z', 1, 3), ('z', 2, 3), ('z', 3, 3), ('z', 4, 3), ('z', 7, 0), ('z', 5, 3), ('z', 6, 3),
    ('f', 0), ('f', 1), ('f', 2), ('f', 3), ('f', 4), ('x', 3), ('z', 7, 1), ('f', 5),
    ('f', 6), ('y', 1, 0, 4), ('z', 7, 2), ('z', 7, 3), ('f', 7), ('y', 0, 1, 4), ('x', 4), ('c', 10),
    ('c', 12), ('z', 10, 0), ('z', 12, 0), ('c', 8), ('z', 10, 1), ('c', 13), ('z', 12, 1), ('z', 8, 0),
    ('z', 10, 2), ('z', 13, 0), ('z', 12, 2), ('z', 8, 1), ('z', 10, 3), ('z', 13, 1), ('y', 0, 0, 3), ('y', 1, 0, 3),
    ('y', 0, 1, 3), ('y', 1, 1, 3), ('c', 16), ('z', 12, 3), ('c', 17), ('z', 8, 2), ('c', 22), ('f', 10),
    ('z', 13, 2), ('z', 16, 0), ('f', 12), ('x', 5), ('z', 17, 0), ('z', 8, 3), ('z', 22, 0), ('z', 13, 3),
    ('z', 16, 1), ('z', 17, 1), ('f', 8), ('z', 22, 1), ('c', 18), ('f', 13), ('y', 1, 1, 4), ('z', 16, 2),
    ('c', 14), ('z', 17, 2), ('c', 20), ('z', 18, 0), ('z', 22, 2), ('z', 16, 3), ('z', 14, 0), ('z', 17, 3),
    ('z', 20, 0), ('z', 18, 1), ('z', 22, 3), ('f', 16), ('c', 11), ('z', 14, 1), ('c', 21), ('z', 20, 1),
    ('f', 17), ('z', 18, 2), ('f', 22), ('c', 15), ('z', 11, 0), ('z', 14, 2), ('z', 21, 0), ('z', 20, 2),
    ('z', 18, 3), ('c', 9), ('z', 11, 1), ('z', 15, 0), ('c', 19), ('z', 14, 3), ('z', 21, 1), ('c', 23),
    ('z', 20, 3), ('f', 18), ('z', 9, 0), ('m', 0, 0), ('z', 11, 2), ('m', 1, 0), ('z', 15, 1), ('z', 19, 0),
    ('f', 14), ('z', 23, 0), ('z', 21, 2), ('f', 20), ('z', 9, 1), ('z', 11, 3), ('z', 15, 2), ('z', 19, 1),
    ('z', 23, 1), ('z', 21, 3), ('z', 9, 2), ('f', 11), ('own',), ('self',), ('z', 15, 3), ('z', 19, 2),
    ('z', 23, 2), ('f', 21), ('z', 9, 3), ('f', 15), ('z', 19, 3), ('z', 23, 3), ('m', 0, 1), ('f', 9),
    ('m', 2, 0), ('f', 19), ('f', 23), ('m', 1, 1), ('next',), ('m', 2, 1), ('far',),
)


def kernel(scale, a_ref, out_ref, G, Q, QP, RL, T, CR, ZR, R, PR, D, O1, O2, MB, MT, MO, OUT,
           xs, xr, ys, yr, cs, cr, zs, zr, ds, dr, ms, mr, ts, tr, os):
    col, tok = lax.axis_index("col"), lax.axis_index("tok")
    lo, y = col // 4, col % 4
    z, hi, c = tok // 4, (tok // 2) % 2, tok % 2
    x = 2 * hi + lo
    s = y // 2

    def at(x_, y_, z_, c_):
        return ((x_ % 2) * 4 + y_, z_ * 4 + (x_ // 2) * 2 + c_)

    x_next, x_prev, x_opposite = (x + 1) % 4, (x + 3) % 4, (x + 2) % 4
    y_next, y_prev, y_far = (y + 1) % 4, (y + 3) % 4, (y + 2) % 4
    x_dev = (at(x_next, y, z, c), at(x_prev, y, z, c))
    x_from = (x_prev, x_next)
    y_up, y_down = at(x, y_next, z, c), at(x, y_prev, z, c)
    sibling = at(x, y, z, 1 - c)
    z_dev = (at(x, y, (z + 1) % 8, c), at(x, y, (z + 7) % 8, c))
    far_lo = (lo + s) % 2
    half_lo = {"p": lo, "r": lo, "0": 1 - lo, "1": 1 - lo, "f": far_lo, "g": far_lo}
    half_h = {"p": hi, "r": 1 - hi, "0": 0, "1": 1, "f": hi, "g": 1 - hi}

    def send(src, dst, s_sem, r_sem, dev):
        cp = pltpu.make_async_remote_copy(src_ref=src, dst_ref=dst, send_sem=s_sem, recv_sem=r_sem,
                                          device_id=dev, device_id_type=MESH)
        cp.start()

    def taken(ref, sem):
        pltpu.make_async_copy(ref, ref, sem).wait()

    partners = [at(2 * (hi ^ dh) + (lo ^ dl), y, z, c ^ dc)
                for dh in range(2) for dl in range(2) for dc in range(2) if dh + dl + dc]
    partners += [at(x, y, (z + dz) % 8, c) for dz in range(1, 8)]
    partners += [at(x, (y + dy) % 4, z, c) for dy in range(1, 4)]
    barrier = pltpu.get_barrier_semaphore()
    for dev in partners:
        pl.semaphore_signal(barrier, inc=1, device_id=dev, device_id_type=MESH)

    def reorder(h, part):
        p = lax.broadcasted_iota(jnp.int32, (BLOCK, HALF), 1)
        f = lax.broadcasted_iota(jnp.int32, (BLOCK, HALF), 0)
        feature = ((p // PART) % 8) * 128 + h * 64 + ((p // 128) % 2) * 32 + (p // CH) * PART + p % PART
        pick = (f == feature).astype(F32).astype(BF16)
        rows = pl.ds(part * HALF, HALF)
        v = jnp.dot(a_ref[rows, :], pick, preferred_element_type=F32).astype(BF16)
        for cc in (A, B):
            G[x, h, cc, rows, :] = v[:, cc * CH:cc * CH + CH]

    def turn(x_, h, cc, dst):
        r = lax.broadcasted_iota(jnp.int32, (CH, CH), 0)
        f = lax.broadcasted_iota(jnp.int32, (CH, CH), 1)
        one = (r == f).astype(F32).astype(BF16)
        dst[...] = lax.dot_general(one, G[x_, h, cc], LAST, preferred_element_type=F32).astype(BF16)

    def h_of(x_):
        return x_ // 2

    def x_sent(n, d):
        b = x_from[d]
        return {0: (x, 1 - hi, A, d), 1: (b, 1 - h_of(b), A, d), 2: (x, 1 - hi, B, d), 3: (b, 1 - h_of(b), B, d),
                4: (x, hi, A, d), 5: (x, 0, A, 1 - d), 6: (x, 1, A, 1 - d), 7: (b, h_of(b), A, d),
                8: (x, hi, B, d), 9: (x, 0, B, 1 - d), 10: (x, 1, B, 1 - d), 11: (b, h_of(b), B, d)}[n]

    def x_unit(x_, h, cc, part):
        return G.at[x_, h, cc, pl.ds(part * HALF, HALF), :]

    def x_send(*messages):
        for n in messages:
            for d in range(2):
                u = x_unit(*x_sent(n, d))
                send(u, u, xs.at[0], xr.at[n], x_dev[d])

    low, high = pl.ds(0, W), pl.ds(W, CH - W)
    slots = (hi, 1 - hi)

    def y_landing(k, r, m):
        q = slots[k]
        return (Q.at[1, q, r, low], Q.at[1, q, r, high], RL.at[2 * k + r], Q.at[2, q, r, low], Q.at[2, q, r, high])[m]

    def y_send(k, r, *messages):
        for m in messages:
            q = slots[k]
            src = (Q.at[0, q, r, low], Q.at[0, q, r, high], Q.at[0, q, r, high], Q.at[1, q, r, low], RL.at[2 * k + r])[m]
            send(src, y_landing(k, r, m), ys.at[m], yr.at[2 * k + r, m], y_down if m in (0, 1, 3) else y_up)

    waited = set()

    def need_x(*messages):
        for n in messages:
            if ("x", n) not in waited:
                waited.add(("x", n))
                taken(G.at[0, 0, 0], xr.at[n])

    def need_y(k, r, *messages):
        for m in messages:
            if ("y", k, r, m) not in waited:
                waited.add(("y", k, r, m))
                taken(y_landing(k, r, m), yr.at[2 * k + r, m])

    def x_step(n):
        if n == 1:
            need_x(0)
            x_send(1, 4, 2, 5)
        elif n == 2:
            need_x(1)
            turn(x_opposite, hi, A, Q.at[0, 1 - hi, A])
            y_send(1, A, 0, 2, 1)
            y_send(0, B, 0, 2, 1)
        elif n == 3:
            need_x(2, 4)
            x_send(3, 6, 7, 8, 9, 10)
        elif n == 4:
            need_x(3)
            turn(x_opposite, hi, B, Q.at[0, 1 - hi, B])
            y_send(1, B, 0, 2, 1)
        else:
            need_x(8)
            x_send(11)

    def y_step(k, r, m):
        need_y(k, r, 0 if m == 3 else 2)
        y_send(k, r, m)

    def compute(cell):
        for j, (kind, r, half, cc) in enumerate(CELLS[cell]):
            l, h = half_lo[half], half_h[half]
            if kind in (OWN, PEER):
                rows = QP[r] if kind == PEER else Q[0, hi, r]
                acc = jnp.dot(rows, G[x, h, cc], preferred_element_type=F32)
            else:
                need_x(*X_NEEDS[half, cc])
                for k in range(2):
                    need_y(k, r, *((), (0, 1), (3, 4))[kind - SELF])
                acc = jnp.dot(Q[kind - SELF, 0, r], G[l, h, cc], preferred_element_type=F32)
                acc += jnp.dot(Q[kind - SELF, 1, r], G[2 + l, h, cc], preferred_element_type=F32)
            T[cell, :, :, :, j * CH:j * CH + CH] = acc.reshape(2, 8, PART, CH)
        send(T.at[cell, 1 - c], CR.at[cell], cs.at[0], cr.at[cell], sibling)

    sides = (pl.ds(0, CH), pl.ds(CH, CH))

    def z_landed(cell, step):
        taken(ZR.at[cell, :, step] if step else ZR.at[cell, 0, 0], zr.at[cell, step])

    def z_step(cell, step):
        if step == 0:
            taken(CR.at[cell], cr.at[cell])
        else:
            z_landed(cell, step - 1)
        for d in range(2):
            to = (z + 4 - step) % 8 if d == 0 else (z + 4 + step) % 8
            if step == 0:
                cols = sides[d]
                T[cell, c, to, :, cols] = T[cell, c, to, :, cols] + CR[cell, to, :, cols]
                send(T.at[cell, c, to, :, cols], ZR.at[cell, d, 0, :, cols], zs.at[0], zr.at[cell, 0], z_dev[d])
                continue
            if step == 1:
                cols, rest = sides[d], sides[1 - d]
                T[cell, c, to, :, cols] = T[cell, c, to, :, cols] + CR[cell, to, :, cols] + ZR[cell, d, 0, :, cols]
                T[cell, c, to, :, rest] = T[cell, c, to, :, rest] + CR[cell, to, :, rest]
            else:
                T[cell, c, to] = T[cell, c, to] + CR[cell, to] + ZR[cell, d, step - 1]
            send(T.at[cell, c, to], ZR.at[cell, d, step], zs.at[0], zr.at[cell, step], z_dev[d])

    def out_cols(l, y_):
        return pl.ds(pl.multiple_of((l * 4 + y_) * BLOCK, BLOCK), BLOCK)

    def group(j, k):
        return pl.ds(pl.multiple_of(j * CH + k * 128, 128), 128)

    def mirror_self(half, k):
        return "no" if k else {"p": "yes", "f": "some"}.get(half, "no")

    def finish(cell):
        z_landed(cell, 3)
        R[cell] = T[cell, c, z] + CR[cell, z] + ZR[cell, 0, 3] + ZR[cell, 1, 3]
        for j, (kind, r, half, cc) in enumerate(CELLS[cell]):
            l, h = half_lo[half], half_h[half]
            cols = pl.ds(j * CH, CH)
            src = R.at[cell, :, cols]
            if kind in (OWN, SELF):
                D[l, h, cc, r] = R[cell, :, cols]
                continue
            if kind == PEER:
                send(src, PR.at[h, cc, r], ds.at[0], dr.at[0], at(x_opposite, y, z, c))
                continue
            if kind == NEXT:
                send(src, O1.at[l, h, cc, r], ds.at[1], dr.at[1], y_up)
            else:
                send(src, O2.at[h, cc, r], ds.at[2], dr.at[2], at(x, y_far, z, c))
            mine = (8 if kind == FAR else lo * 4) + hi * 2 + c
            s_sem, batch = ms.at[kind - NEXT], 2 if kind == FAR else 1 if half in "pr" else 0
            for dk in range(2):
                k = (c + dk) % 2
                part, dst, dev = R.at[cell, :, group(j, k)], MB.at[cc, mine, r], at(2 * h + l, y, z, k)
                stays = mirror_self(half, dk)

                def leave():
                    send(part, dst, s_sem, mr.at[batch, cc], dev)

                def keep():
                    MB[cc, mine, r] = R[cell, :, group(j, k)]
                if stays == "no":
                    leave()
                elif stays == "yes":
                    keep()
                else:
                    pl.when(s == 0)(keep)
                    pl.when(s == 1)(leave)

    mirror_base = ((1 - lo) * 4, lo * 4, 8)

    def mirror(b, cc):
        def take(n):
            taken(MB.at[cc, 0:n], mr.at[b, cc])
        if b < 2:
            take(4 - b)
        else:
            pl.when(s == 0)(lambda: take(3))
            pl.when(s == 1)(lambda: take(4))
        turned = jnp.transpose(MB[cc, pl.ds(mirror_base[b], 4)].reshape(4 * ROWS, 4 * ROWS))
        MT[b, cc] = turned.reshape(8, PART, 4 * ROWS) * scale
        MO[b, z, cc] = MT[b, cc, z]
        for dz in range(1, 8):
            to = (z + dz) % 8
            send(MT.at[b, cc, to], MO.at[b, z, cc], ts.at[0], tr.at[b, cc], at(x, y, to, c))

    def store(n, l, y_, v):
        OUT[n] = v
        pltpu.make_async_copy(OUT.at[n], out_ref.at[:, out_cols(l, y_)], os.at[0]).start()

    def natural(v):
        t = [[v[h, cc].reshape(ROWS, CH) for cc in (A, B)] for h in range(2)]
        return scale * jnp.concatenate([t[h][cc][:, k * 128 + b * PART:k * 128 + b * PART + PART]
                                        for b in range(8) for h in range(2) for k in range(2) for cc in (A, B)], axis=1)

    def store_mirror(b, l, y_):
        for cc in (A, B):
            taken(MO.at[b, 0:7, cc], tr.at[b, cc])
        store(5 + b, l, y_, jnp.concatenate([MO[b, k].reshape(ROWS, 4 * ROWS) for k in range(8)], axis=1))

    def store_own():
        taken(PR, dr.at[0])
        store(0, lo, y, natural(D[lo] + PR[...]))

    def store_next():
        taken(O1, dr.at[1])
        for l in range(2):
            store(1 + l, l, y_prev, natural(O1[l]))

    def store_far():
        taken(O2, dr.at[2])
        store(3, (lo + 1 - s) % 2, y_far, natural(O2[...]))

    def store_self():
        store(4, 1 - lo, y, natural(D[1 - lo]))

    for part in range(2):
        reorder(1 - hi, part)
    pl.semaphore_wait(barrier, len(partners))
    x_send(0)
    for part in range(2):
        reorder(hi, part)
    turn(x, hi, A, Q.at[0, hi, A])
    y_send(0, A, 0, 2, 1)
    turn(x, hi, B, Q.at[0, hi, B])
    for cc in (A, B):
        turn(x, 1 - hi, cc, QP.at[cc])

    steps = {"x": x_step, "y": y_step, "c": compute, "z": z_step, "f": finish, "m": mirror, "own": store_own, "next": store_next,
             "far": store_far, "self": store_self}
    for name, *given in ORDER:
        steps[name](*given)
    store_mirror(0, 1 - lo, y_next)
    store_mirror(1, lo, y_next)
    store_mirror(2, far_lo, y_far)

    taken(G.at[0:3], xs.at[0])
    for m in range(5):
        taken(Q.at[0, :, :, low if m in (0, 3) else high], ys.at[m])
    taken(CR, cs.at[0])
    taken(CR.at[0:COUNT * 7 // 8], zs.at[0])
    for n, ref in enumerate((PR, O1, O2)):
        taken(ref, ds.at[n])
    taken(MB.at[:, 0:7], ms.at[0])
    for v in range(2):
        pl.when(s == v)(lambda: taken(MB.at[:, 0:3 + v], ms.at[1]))
    taken(MT.at[:, :, 0:7], ts.at[0])
    taken(OUT, os.at[0])


def solution(mesh):
    token_ranks = mesh.shape["tok"]

    def shards(activations):
        scale = 1.0 / (activations.shape[0] * token_ranks)
        dma = pltpu.SemaphoreType.DMA
        return pl.pallas_call(
            lambda *refs: kernel(scale, *refs),
            out_shape=jax.ShapeDtypeStruct((ROWS, 8 * BLOCK), F32),
            in_specs=[pl.BlockSpec(memory_space=pltpu.VMEM)],
            out_specs=pl.BlockSpec(memory_space=pl.ANY),
            scratch_shapes=[
                pltpu.VMEM((4, 2, 2, BLOCK, CH), BF16),
                pltpu.VMEM((3, 2, 2, CH, BLOCK), BF16),
                pltpu.VMEM((2, CH, BLOCK), BF16),
                pltpu.VMEM((4, CH - W, BLOCK), BF16),
                pltpu.VMEM((COUNT, 2, 8, PART, HALF), F32),
                pltpu.VMEM((COUNT, 8, PART, HALF), F32),
                pltpu.VMEM((COUNT, 2, 4, PART, HALF), F32),
                pltpu.VMEM((COUNT, PART, HALF), F32),
                pltpu.VMEM((2, 2, 2, PART, CH), F32),
                pltpu.VMEM((2, 2, 2, 2, PART, CH), F32),
                pltpu.VMEM((2, 2, 2, 2, PART, CH), F32),
                pltpu.VMEM((2, 2, 2, PART, CH), F32),
                pltpu.VMEM((2, 12, 2, PART, 4 * ROWS), F32),
                pltpu.VMEM((3, 2, 8, PART, 4 * ROWS), F32),
                pltpu.VMEM((3, 8, 2, PART, 4 * ROWS), F32),
                pltpu.VMEM((8, ROWS, BLOCK), F32),
                dma((1,)), dma((12,)),
                dma((5,)), dma((4, 5)),
                dma((1,)), dma((COUNT,)),
                dma((1,)), dma((COUNT, 4)),
                dma((3,)), dma((3,)),
                dma((2,)), dma((3, 2)),
                dma((1,)), dma((3, 2)),
                dma((1,)),
            ],
            compiler_params=pltpu.CompilerParams(
                collective_id=0, has_side_effects=True, vmem_limit_bytes=56 * 1024 * 1024),
            cost_estimate=pl.CostEstimate(flops=14 * 10**9, bytes_accessed=3 * 2**20, transcendentals=0),
            name="gram",
        )(activations)

    return jax.shard_map(shards, mesh=mesh, in_specs=(P("tok", "col"),), out_specs=P(("col", "tok"), None), check_vma=False)
```

```python
import jax
import jax.numpy as jnp
from jax import lax
from jax.experimental import pallas as pl
from jax.experimental.pallas import tpu as pltpu
from jax.sharding import PartitionSpec as P

MESH = pl.DeviceIdType.MESH
F32, BF16 = jnp.float32, jnp.bfloat16
BLOCK = 1024
HALF = BLOCK // 2
CH = HALF // 2
ROWS = 32
PART = ROWS // 2
W = 80
LAST = (((1,), (1,)), ((), ()))
A, B = 0, 1
OWN, PEER, SELF, NEXT, FAR = range(5)
CELLS = (
    ((OWN, A, "p", A), (OWN, A, "p", B),),
    ((OWN, A, "r", A), (OWN, A, "r", B),),
    ((OWN, B, "p", A), (OWN, B, "p", B),),
    ((OWN, B, "r", A), (OWN, B, "r", B),),
    ((PEER, A, "p", A), (PEER, A, "p", B),),
    ((PEER, A, "r", A), (PEER, A, "r", B),),
    ((PEER, B, "p", A), (PEER, B, "p", B),),
    ((PEER, B, "r", A), (PEER, B, "r", B),),
    ((FAR, B, "g", A),),
    ((NEXT, A, "r", B), (FAR, B, "f", B),),
    ((SELF, B, "u", B), (NEXT, B, "r", A),),
    ((NEXT, A, "p", A),),
    ((NEXT, A, "1", B), (NEXT, A, "r", A),),
    ((SELF, B, "u", A),),
    ((NEXT, B, "1", B),),
    ((SELF, A, "u", B), (FAR, A, "f", B),),
    ((NEXT, B, "p", B), (NEXT, B, "1", A),),
    ((NEXT, B, "r", B),),
    ((NEXT, A, "1", A), (NEXT, A, "p", B),),
    ((FAR, A, "g", B),),
    ((FAR, A, "g", A),),
    ((FAR, A, "f", A),),
    ((FAR, B, "g", B),),
    ((NEXT, B, "p", A),),
    ((FAR, B, "f", A),),
    ((SELF, A, "u", A), (NEXT, A, "0", B),),
    ((NEXT, A, "0", A), (NEXT, B, "0", A),),
    ((NEXT, B, "0", B),),
)
COUNT = len(CELLS)
PAIRS = sum(len(tiles) for tiles in CELLS) // 2
X_NEEDS = {("p", A): (1,), ("p", B): (3,), ("r", A): (7,), ("r", B): (11,), ("0", A): (0, 4, 5), ("0", B): (2, 8, 9),
           ("1", A): (0, 4, 6), ("1", B): (2, 8, 10), ("f", A): (1, 0, 4, 5, 6), ("f", B): (3, 2, 8, 9, 10),
           ("g", A): (7, 0, 4, 5, 6), ("g", B): (11, 2, 8, 9, 10), ("u", A): (0, 4, 5, 6), ("u", B): (2, 8, 9, 10)}
X_FORWARD = {1: 0, 3: 2, 7: 4, 11: 8}
X_GROUPS = ((0, 2), (1, 6, 5), (3, 4, 8, 9, 10), (7,), (11,))
OWN_FIRST = True

ORDER = (
    ('c', 0), ('c', 1), ('c', 2), ('c', 3), ('c', 4), ('c', 5), ('c', 6), ('z', 0, 0),
    ('c', 7), ('z', 1, 0), ('z', 2, 0), ('x', 1), ('z', 3, 0), ('z', 4, 0), ('z', 5, 0), ('z', 6, 0),
    ('z', 0, 1), ('z', 7, 0), ('z', 1, 1), ('z', 2, 1), ('z', 3, 1), ('z', 4, 1), ('z', 5, 1), ('y', 0, 0, 4),
    ('z', 6, 1), ('z', 0, 2), ('z', 7, 1), ('x', 2), ('z', 1, 2), ('z', 2, 2), ('z', 3, 2), ('z', 4, 2),
    ('z', 5, 2), ('z', 6, 2), ('z', 0, 3), ('z', 7, 2), ('t', 0), ('y', 0, 1, 4), ('z', 1, 3), ('z', 2, 3),
    ('z', 3, 3), ('z', 4, 3), ('z', 5, 3), ('z', 6, 3), ('f', 0), ('z', 7, 3), ('f', 1), ('f', 2),
    ('f', 3), ('f', 4), ('f', 5), ('f', 6), ('f', 7), ('y', 1, 0, 4), ('t', 1), ('y', 0, 0, 3),
    ('y', 1, 0, 3), ('y', 0, 1, 3), ('c', 11), ('z', 11, 0), ('x', 3), ('c', 13), ('y', 1, 1, 3), ('c', 18),
    ('z', 11, 1), ('z', 13, 0), ('z', 18, 0), ('z', 11, 2), ('z', 13, 1), ('x', 4), ('peer',), ('z', 18, 1),
    ('z', 11, 3), ('c', 16), ('z', 13, 2), ('c', 23), ('c', 26), ('z', 18, 2), ('z', 16, 0), ('c', 25),
    ('z', 13, 3), ('z', 23, 0), ('c', 27), ('z', 26, 0), ('z', 18, 3), ('z', 16, 1), ('z', 25, 0), ('c', 21),
    ('z', 23, 1), ('z', 26, 1), ('z', 27, 0), ('y', 1, 1, 4), ('f', 11), ('f', 13), ('f', 18), ('c', 14),
    ('z', 16, 2), ('c', 15), ('z', 21, 0), ('z', 23, 2), ('z', 25, 1), ('z', 26, 2), ('z', 27, 1), ('z', 14, 0),
    ('z', 16, 3), ('z', 15, 0), ('z', 21, 1), ('z', 23, 3), ('z', 25, 2), ('z', 26, 3), ('c', 10), ('z', 14, 1),
    ('z', 27, 2), ('c', 12), ('z', 15, 1), ('c', 20), ('z', 21, 2), ('f', 16), ('f', 23), ('z', 25, 3),
    ('z', 10, 0), ('c', 8), ('c', 24), ('z', 14, 2), ('z', 12, 0), ('f', 26), ('z', 27, 3), ('z', 20, 0),
    ('z', 15, 2), ('z', 21, 3), ('c', 9), ('z', 8, 0), ('z', 10, 1), ('z', 24, 0), ('c', 17), ('z', 14, 3),
    ('z', 12, 1), ('c', 19), ('c', 22), ('z', 20, 1), ('f', 25), ('f', 27), ('z', 15, 3), ('f', 21),
    ('z', 9, 0), ('z', 8, 1), ('z', 17, 0), ('z', 10, 2), ('z', 24, 1), ('z', 19, 0), ('f', 14), ('z', 22, 0),
    ('z', 12, 2), ('z', 20, 2), ('f', 15), ('z', 9, 1), ('m', 0, 0), ('z', 8, 2), ('z', 17, 1), ('z', 10, 3),
    ('z', 24, 2), ('z', 19, 1), ('z', 22, 1), ('z', 12, 3), ('z', 20, 3), ('z', 9, 2), ('z', 8, 3), ('z', 17, 2),
    ('f', 10), ('z', 24, 3), ('z', 19, 2), ('z', 22, 2), ('f', 12), ('f', 20), ('z', 9, 3), ('f', 8),
    ('z', 17, 3), ('f', 24), ('z', 19, 3), ('z', 22, 3), ('u',), ('f', 9), ('f', 17), ('m', 0, 1),
    ('m', 1, 0), ('f', 19), ('f', 22), ('m', 2, 0), ('m', 1, 1), ('own',), ('self',), ('next',),
    ('m', 2, 1), ('far',),
)


def kernel(scale, a_ref, out_ref, G, Q, QP, RL, T, CR, ZR, R, PR, D, O1, O2, MB, MT, MO, DU, MTU, MOU, OUT,
           xs, xr, ys, yr, cs, cr, zs, zr, ds, dr, ms, mr, ts, tr, os):
    col, tok = lax.axis_index("col"), lax.axis_index("tok")
    lo, y = col // 4, col % 4
    z, hi, c = tok // 4, (tok // 2) % 2, tok % 2
    x = 2 * hi + lo
    s = y // 2

    def at(x_, y_, z_, c_):
        return ((x_ % 2) * 4 + y_, z_ * 4 + (x_ // 2) * 2 + c_)

    x_next, x_prev, x_opposite = (x + 1) % 4, (x + 3) % 4, (x + 2) % 4
    y_next, y_prev, y_far = (y + 1) % 4, (y + 3) % 4, (y + 2) % 4
    x_dev = (at(x_next, y, z, c), at(x_prev, y, z, c))
    x_from = (x_prev, x_next)
    y_up, y_down = at(x, y_next, z, c), at(x, y_prev, z, c)
    sibling = at(x, y, z, 1 - c)
    z_dev = (at(x, y, (z + 1) % 8, c), at(x, y, (z + 7) % 8, c))
    far_lo = (lo + s) % 2
    half_lo = {"p": lo, "r": lo, "0": 1 - lo, "1": 1 - lo, "f": far_lo, "g": far_lo, "u": 1 - lo}
    half_h = {"p": hi, "r": 1 - hi, "0": 0, "1": 1, "f": hi, "g": 1 - hi, "u": x_next // 2}

    def send(src, dst, s_sem, r_sem, dev):
        cp = pltpu.make_async_remote_copy(src_ref=src, dst_ref=dst, send_sem=s_sem, recv_sem=r_sem,
                                          device_id=dev, device_id_type=MESH)
        cp.start()

    def taken(ref, sem):
        pltpu.make_async_copy(ref, ref, sem).wait()

    partners = [at(2 * (hi ^ dh) + (lo ^ dl), y, z, c ^ dc)
                for dh in range(2) for dl in range(2) for dc in range(2) if dh + dl + dc]
    partners += [at(x, y, (z + dz) % 8, c) for dz in range(1, 8)]
    partners += [at(x, (y + dy) % 4, z, c) for dy in range(1, 4)]
    barrier = pltpu.get_barrier_semaphore()
    for dev in partners:
        pl.semaphore_signal(barrier, inc=1, device_id=dev, device_id_type=MESH)

    def reorder(h, part):
        p = lax.broadcasted_iota(jnp.int32, (BLOCK, HALF), 1)
        f = lax.broadcasted_iota(jnp.int32, (BLOCK, HALF), 0)
        feature = ((p // PART) % 8) * 128 + h * 64 + ((p // 128) % 2) * 32 + (p // CH) * PART + p % PART
        pick = (f == feature).astype(F32).astype(BF16)
        rows = pl.ds(part * HALF, HALF)
        v = jnp.dot(a_ref[rows, :], pick, preferred_element_type=F32).astype(BF16)
        for cc in (A, B):
            G[x, h, cc, rows, :] = v[:, cc * CH:cc * CH + CH]

    def turn(x_, h, cc, dst):
        r = lax.broadcasted_iota(jnp.int32, (CH, CH), 0)
        f = lax.broadcasted_iota(jnp.int32, (CH, CH), 1)
        one = (r == f).astype(F32).astype(BF16)
        dst[...] = lax.dot_general(one, G[x_, h, cc], LAST, preferred_element_type=F32).astype(BF16)

    def h_of(x_):
        return x_ // 2

    def x_sent(n, d):
        b = x_from[d]
        return {0: (x, 1 - hi, A, d), 1: (b, 1 - h_of(b), A, d), 2: (x, 1 - hi, B, d), 3: (b, 1 - h_of(b), B, d),
                4: (x, hi, A, d), 5: (x, 0, A, 1 - d), 6: (x, 1, A, 1 - d), 7: (b, h_of(b), A, d),
                8: (x, hi, B, d), 9: (x, 0, B, 1 - d), 10: (x, 1, B, 1 - d), 11: (b, h_of(b), B, d)}[n]

    def x_unit(x_, h, cc, part):
        return G.at[x_, h, cc, pl.ds(part * HALF, HALF), :]

    def x_send(*messages):
        for n in messages:
            for d in range(2):
                u = x_unit(*x_sent(n, d))
                send(u, u, xs.at[0], xr.at[n], x_dev[d])

    low, high = pl.ds(0, W), pl.ds(W, CH - W)
    slots = (hi, 1 - hi)

    def y_landing(k, r, m):
        q = slots[k]
        return (Q.at[1, q, r, low], Q.at[1, q, r, high], RL.at[2 * k + r], Q.at[2, q, r, low], Q.at[2, q, r, high])[m]

    def y_send(k, r, *messages):
        for m in messages:
            q = slots[k]
            src = (Q.at[0, q, r, low], Q.at[0, q, r, high], Q.at[0, q, r, high], Q.at[1, q, r, low], RL.at[2 * k + r])[m]
            send(src, y_landing(k, r, m), ys.at[m], yr.at[2 * k + r, m], y_down if m in (0, 1, 3) else y_up)

    waited = set()

    def need_x(*messages):
        for n in messages:
            if ("x", n) not in waited:
                waited.add(("x", n))
                taken(G.at[0, 0, 0], xr.at[n])

    def need_y(k, r, *messages):
        for m in messages:
            if ("y", k, r, m) not in waited:
                waited.add(("y", k, r, m))
                taken(y_landing(k, r, m), yr.at[2 * k + r, m])

    def x_step(n):
        if n:
            need_x(X_FORWARD[X_GROUPS[n][0]])
        x_send(*X_GROUPS[n])

    def q_step(r):
        need_x((1, 3)[r])
        turn(x_opposite, hi, r, Q.at[0, 1 - hi, r])
        y_send(1, r, 0, 2, 1)
        if r == A and not OWN_FIRST:
            y_send(0, B, 0, 2, 1)

    def y_step(k, r, m):
        need_y(k, r, 0 if m == 3 else 2)
        y_send(k, r, m)

    def compute(cell):
        for j, (kind, r, half, cc) in enumerate(CELLS[cell]):
            l, h = half_lo[half], half_h[half]
            if kind in (OWN, PEER):
                rows = QP[r] if kind == PEER else Q[0, hi, r]
                acc = jnp.dot(rows, G[x, h, cc], preferred_element_type=F32)
            else:
                need_x(*X_NEEDS[half, cc])
                for k in range(2):
                    need_y(k, r, *((), (0, 1), (3, 4))[kind - SELF])
                acc = jnp.dot(Q[kind - SELF, 0, r], G[l, h, cc], preferred_element_type=F32)
                acc += jnp.dot(Q[kind - SELF, 1, r], G[2 + l, h, cc], preferred_element_type=F32)
            T[cell, :, :, :, j * CH:j * CH + CH] = acc.reshape(2, 8, PART, CH)
        w = width(cell)
        send(T.at[cell, 1 - c, :, :, w], CR.at[cell, :, :, w], cs.at[0], cr.at[cell], sibling)

    def width(cell):
        return pl.ds(0, CH * len(CELLS[cell]))

    def z_landed(cell, step):
        w = width(cell)
        taken(ZR.at[cell, :, step, :, w] if step else ZR.at[cell, 0, 0, :, w], zr.at[cell, step])

    def z_step(cell, step):
        w, n = width(cell), CH * len(CELLS[cell]) // 2
        sides = (pl.ds(0, n), pl.ds(n, n))
        if step == 0:
            taken(CR.at[cell, :, :, w], cr.at[cell])
        else:
            z_landed(cell, step - 1)
        for d in range(2):
            to = (z + 4 - step) % 8 if d == 0 else (z + 4 + step) % 8
            if step == 0:
                cols = sides[d]
                T[cell, c, to, :, cols] = T[cell, c, to, :, cols] + CR[cell, to, :, cols]
                send(T.at[cell, c, to, :, cols], ZR.at[cell, d, 0, :, cols], zs.at[0], zr.at[cell, 0], z_dev[d])
                continue
            if step == 1:
                cols, rest = sides[d], sides[1 - d]
                T[cell, c, to, :, cols] = T[cell, c, to, :, cols] + CR[cell, to, :, cols] + ZR[cell, d, 0, :, cols]
                T[cell, c, to, :, rest] = T[cell, c, to, :, rest] + CR[cell, to, :, rest]
            else:
                T[cell, c, to, :, w] = T[cell, c, to, :, w] + CR[cell, to, :, w] + ZR[cell, d, step - 1, :, w]
            send(T.at[cell, c, to, :, w], ZR.at[cell, d, step, :, w], zs.at[0], zr.at[cell, step], z_dev[d])

    def out_cols(l, y_):
        return pl.ds(pl.multiple_of((l * 4 + y_) * BLOCK, BLOCK), BLOCK)

    def group(j, k):
        return pl.ds(pl.multiple_of(j * CH + k * 128, 128), 128)

    def mirror_self(half, k):
        return "no" if k else {"p": "yes", "f": "some"}.get(half, "no")

    def finish(cell):
        z_landed(cell, 3)
        w = width(cell)
        R[cell, :, w] = T[cell, c, z, :, w] + CR[cell, z, :, w] + ZR[cell, 0, 3, :, w] + ZR[cell, 1, 3, :, w]
        for j, (kind, r, half, cc) in enumerate(CELLS[cell]):
            l, h = half_lo[half], half_h[half]
            cols = pl.ds(j * CH, CH)
            src = R.at[cell, :, cols]
            if kind == OWN:
                D[h, cc, r] = R[cell, :, cols]
                continue
            if kind == SELF:
                DU[cc, r] = R[cell, :, cols]
                for k in range(2):
                    send(R.at[cell, :, pl.ds(j * CH + k * 128, 128)], MB.at[cc, 12 + c, r], ms.at[2], mr.at[3, 0],
                         at(x_next, y, z, k))
                continue
            if kind == PEER:
                continue
            if kind == NEXT:
                send(src, O1.at[l, h, cc, r], ds.at[1], dr.at[1], y_up)
            else:
                send(src, O2.at[h, cc, r], ds.at[2], dr.at[2], at(x, y_far, z, c))
            mine = (8 if kind == FAR else lo * 4) + hi * 2 + c
            s_sem, batch = ms.at[kind - NEXT], 2 if kind == FAR else 1 if half in "pr" else 0
            for dk in range(2):
                k = (c + dk) % 2
                part, dst, dev = R.at[cell, :, group(j, k)], MB.at[cc, mine, r], at(2 * h + l, y, z, k)
                stays = mirror_self(half, dk)

                def leave():
                    send(part, dst, s_sem, mr.at[batch, cc], dev)

                def keep():
                    MB[cc, mine, r] = R[cell, :, group(j, k)]
                if stays == "no":
                    leave()
                elif stays == "yes":
                    keep()
                else:
                    pl.when(s == 0)(keep)
                    pl.when(s == 1)(leave)

    def send_peer():
        for cell, tiles in enumerate(CELLS):
            for j, (kind, r, half, cc) in enumerate(tiles):
                if kind == PEER:
                    send(R.at[cell, :, pl.ds(j * CH, CH)], PR.at[half_h[half], cc, r], ds.at[0], dr.at[0], at(x_opposite, y, z, c))

    mirror_base = ((1 - lo) * 4, lo * 4, 8)

    def mirror(b, cc):
        def take(n):
            taken(MB.at[cc, 0:n], mr.at[b, cc])
        if b < 2:
            take(4 - b)
        else:
            pl.when(s == 0)(lambda: take(3))
            pl.when(s == 1)(lambda: take(4))
        turned = jnp.transpose(MB[cc, pl.ds(mirror_base[b], 4)].reshape(4 * ROWS, 4 * ROWS))
        MT[b, cc] = turned.reshape(8, PART, 4 * ROWS) * scale
        MO[b, z, cc] = MT[b, cc, z]
        for dz in range(1, 8):
            to = (z + dz) % 8
            send(MT.at[b, cc, to], MO.at[b, z, cc], ts.at[0], tr.at[b, cc], at(x, y, to, c))

    def mirror_next_x():
        taken(MB.at[0, 0:4], mr.at[3, 0])
        turned = [jnp.transpose(MB[cc, 12:14].reshape(2 * ROWS, 4 * ROWS)).reshape(8, PART, 2 * ROWS) for cc in (A, B)]
        MTU[...] = jnp.concatenate(turned, axis=2) * scale
        MOU[z] = MTU[z]
        for dz in range(1, 8):
            to = (z + dz) % 8
            send(MTU.at[to], MOU.at[z], ts.at[1], tr.at[3, 0], at(x, y, to, c))

    def store(n, l, y_, v):
        OUT[n] = v
        pltpu.make_async_copy(OUT.at[n], out_ref.at[:, out_cols(l, y_)], os.at[0]).start()

    def natural(v):
        t = [[v[h, cc].reshape(ROWS, CH) for cc in (A, B)] for h in range(2)]
        return scale * jnp.concatenate([t[h][cc][:, k * 128 + b * PART:k * 128 + b * PART + PART]
                                        for b in range(8) for h in range(2) for k in range(2) for cc in (A, B)], axis=1)

    def store_mirror(b, l, y_):
        for cc in (A, B):
            taken(MO.at[b, 0:7, cc], tr.at[b, cc])
        store(5 + b, l, y_, jnp.concatenate([MO[b, k].reshape(ROWS, 4 * ROWS) for k in range(8)], axis=1))

    def store_own():
        taken(PR, dr.at[0])
        store(0, lo, y, natural(D[...] + PR[...]))

    def store_next():
        taken(O1, dr.at[1])
        for l in range(2):
            store(1 + l, l, y_prev, natural(O1[l]))

    def store_far():
        taken(O2, dr.at[2])
        store(3, (lo + 1 - s) % 2, y_far, natural(O2[...]))

    def store_self():
        taken(MOU.at[0:7], tr.at[3, 0])
        direct = [DU[cc].reshape(ROWS, CH) * scale for cc in (A, B)]
        first = x_next // 2 == 0
        groups = []
        for b in range(8):
            own = jnp.concatenate([direct[cc][:, k * 128 + b * PART:k * 128 + b * PART + PART]
                                   for k in range(2) for cc in (A, B)], axis=1)
            other = jnp.concatenate([MOU[b, :, cc * 64:cc * 64 + 64] for cc in (A, B)], axis=0)
            groups += [jnp.where(first, own, other), jnp.where(first, other, own)]
        store(4, 1 - lo, y, jnp.concatenate(groups, axis=1))

    for part in range(2):
        reorder(1 - hi, part)
    pl.semaphore_wait(barrier, len(partners))
    x_step(0)
    for part in range(2):
        reorder(hi, part)
    turn(x, hi, A, Q.at[0, hi, A])
    y_send(0, A, 0, 2, 1)
    turn(x, hi, B, Q.at[0, hi, B])
    if OWN_FIRST:
        y_send(0, B, 0, 2, 1)
    for cc in (A, B):
        turn(x, 1 - hi, cc, QP.at[cc])

    steps = {"x": x_step, "t": q_step, "u": mirror_next_x, "y": y_step, "c": compute, "z": z_step, "f": finish, "m": mirror, "peer": send_peer, "own": store_own, "next": store_next,
             "far": store_far, "self": store_self}
    for name, *given in ORDER:
        steps[name](*given)
    store_mirror(0, 1 - lo, y_next)
    store_mirror(1, lo, y_next)
    store_mirror(2, far_lo, y_far)

    taken(G.at[0:3], xs.at[0])
    for m in range(5):
        taken(Q.at[0, :, :, low if m in (0, 3) else high], ys.at[m])
    taken(CR.at[0:PAIRS], cs.at[0])
    taken(CR.at[0:PAIRS, 0:7], zs.at[0])
    for n, ref in enumerate((PR, O1, O2)):
        taken(ref, ds.at[n])
    taken(MB.at[:, 0:7], ms.at[0])
    for v in range(2):
        pl.when(s == v)(lambda: taken(MB.at[:, 0:3 + v], ms.at[1]))
    taken(MB.at[0, 0:4], ms.at[2])
    taken(MT.at[:, :, 0:7], ts.at[0])
    taken(MTU.at[0:7], ts.at[1])
    taken(OUT, os.at[0])


def solution(mesh):
    token_ranks = mesh.shape["tok"]

    def shards(activations):
        scale = 1.0 / (activations.shape[0] * token_ranks)
        dma = pltpu.SemaphoreType.DMA
        return pl.pallas_call(
            lambda *refs: kernel(scale, *refs),
            out_shape=jax.ShapeDtypeStruct((ROWS, 8 * BLOCK), F32),
            in_specs=[pl.BlockSpec(memory_space=pltpu.VMEM)],
            out_specs=pl.BlockSpec(memory_space=pl.ANY),
            scratch_shapes=[
                pltpu.VMEM((4, 2, 2, BLOCK, CH), BF16),
                pltpu.VMEM((3, 2, 2, CH, BLOCK), BF16),
                pltpu.VMEM((2, CH, BLOCK), BF16),
                pltpu.VMEM((4, CH - W, BLOCK), BF16),
                pltpu.VMEM((COUNT, 2, 8, PART, HALF), F32),
                pltpu.VMEM((COUNT, 8, PART, HALF), F32),
                pltpu.VMEM((COUNT, 2, 4, PART, HALF), F32),
                pltpu.VMEM((COUNT, PART, HALF), F32),
                pltpu.VMEM((2, 2, 2, PART, CH), F32),
                pltpu.VMEM((2, 2, 2, PART, CH), F32),
                pltpu.VMEM((2, 2, 2, 2, PART, CH), F32),
                pltpu.VMEM((2, 2, 2, PART, CH), F32),
                pltpu.VMEM((2, 14, 2, PART, 4 * ROWS), F32),
                pltpu.VMEM((3, 2, 8, PART, 4 * ROWS), F32),
                pltpu.VMEM((3, 8, 2, PART, 4 * ROWS), F32),
                pltpu.VMEM((2, 2, PART, CH), F32),
                pltpu.VMEM((8, PART, 4 * ROWS), F32),
                pltpu.VMEM((8, PART, 4 * ROWS), F32),
                pltpu.VMEM((8, ROWS, BLOCK), F32),
                dma((1,)), dma((12,)),
                dma((5,)), dma((4, 5)),
                dma((1,)), dma((COUNT,)),
                dma((1,)), dma((COUNT, 4)),
                dma((3,)), dma((3,)),
                dma((3,)), dma((4, 2)),
                dma((2,)), dma((4, 2)),
                dma((1,)),
            ],
            compiler_params=pltpu.CompilerParams(
                collective_id=0, has_side_effects=True, vmem_limit_bytes=56 * 1024 * 1024),
            cost_estimate=pl.CostEstimate(flops=14 * 10**9, bytes_accessed=3 * 2**20, transcendentals=0),
            name="gram",
        )(activations)

    return jax.shard_map(shards, mesh=mesh, in_specs=(P("tok", "col"),), out_specs=P(("col", "tok"), None), check_vma=False)
```

```python
import jax
import jax.numpy as jnp
from jax import lax
from jax.experimental import pallas as pl
from jax.experimental.pallas import tpu as pltpu
from jax.sharding import PartitionSpec as P

MESH = pl.DeviceIdType.MESH
F32, BF16 = jnp.float32, jnp.bfloat16
BLOCK = 1024
HALF = BLOCK // 2
CH = HALF // 2
ROWS = 32
PART = ROWS // 2
W = 80
LAST = (((1,), (1,)), ((), ()))
A, B = 0, 1
OWN, PEER, SELF, NEXT, FAR = range(5)
CELLS = (
    ((OWN, A, "p", A), (OWN, A, "p", B),),
    ((OWN, A, "r", A), (OWN, A, "r", B),),
    ((OWN, B, "p", A), (OWN, B, "p", B),),
    ((OWN, B, "r", A), (OWN, B, "r", B),),
    ((PEER, A, "p", A), (PEER, A, "p", B),),
    ((PEER, A, "r", A), (PEER, A, "r", B),),
    ((PEER, B, "p", A), (PEER, B, "p", B),),
    ((PEER, B, "r", A), (PEER, B, "r", B),),
    ((NEXT, A, "0", A), (SELF, B, "u", A),),
    ((NEXT, A, "r", B), (NEXT, B, "r", B),),
    ((FAR, A, "f", B), (NEXT, B, "0", B),),
    ((FAR, A, "g", B), (FAR, B, "g", B),),
    ((SELF, A, "u", B),),
    ((NEXT, A, "1", A),),
    ((NEXT, A, "p", A),),
    ((FAR, B, "f", B),),
    ((NEXT, B, "p", A),),
    ((NEXT, A, "p", B),),
    ((NEXT, B, "r", A), (FAR, B, "g", A),),
    ((NEXT, B, "p", B), (SELF, A, "u", A),),
    ((NEXT, B, "0", A), (SELF, B, "u", B),),
    ((FAR, B, "f", A),),
    ((NEXT, B, "1", B),),
    ((FAR, A, "g", A),),
    ((NEXT, A, "0", B),),
    ((NEXT, A, "1", B), (NEXT, B, "1", A),),
    ((FAR, A, "f", A),),
    ((NEXT, A, "r", A),),
)
COUNT = len(CELLS)
PAIRS = sum(len(tiles) for tiles in CELLS) // 2
X_NEEDS = {("p", A): (1,), ("p", B): (3,), ("r", A): (7,), ("r", B): (11,), ("0", A): (0, 4, 5), ("0", B): (2, 8, 9),
           ("1", A): (0, 4, 6), ("1", B): (2, 8, 10), ("f", A): (1, 0, 4, 5, 6), ("f", B): (3, 2, 8, 9, 10),
           ("g", A): (7, 0, 4, 5, 6), ("g", B): (11, 2, 8, 9, 10), ("u", A): (0, 4, 5, 6), ("u", B): (2, 8, 9, 10)}
X_FORWARD = {1: 0, 3: 2, 7: 4, 11: 8}
X_GROUPS = ((0, 2), (1, 8, 5), (3, 4, 6, 10, 9), (11,), (7,))
OWN_FIRST = True

ORDER = (
    ('c', 0), ('c', 1), ('c', 2), ('c', 3), ('c', 4), ('c', 5), ('c', 6), ('z', 0, 0),
    ('c', 7), ('z', 1, 0), ('z', 2, 0), ('x', 1), ('z', 3, 0), ('z', 4, 0), ('z', 5, 0), ('z', 6, 0),
    ('z', 0, 1), ('z', 7, 0), ('z', 1, 1), ('z', 2, 1), ('z', 3, 1), ('z', 4, 1), ('z', 5, 1), ('y', 0, 0, 4),
    ('z', 6, 1), ('z', 0, 2), ('z', 7, 1), ('x', 2), ('z', 1, 2), ('z', 2, 2), ('z', 3, 2), ('z', 4, 2),
    ('z', 5, 2), ('z', 6, 2), ('z', 0, 3), ('z', 7, 2), ('t', 0), ('y', 0, 1, 4), ('z', 1, 3), ('z', 2, 3),
    ('z', 3, 3), ('z', 4, 3), ('z', 5, 3), ('z', 6, 3), ('f', 0), ('z', 7, 3), ('x', 3), ('f', 1),
    ('f', 2), ('f', 3), ('f', 4), ('f', 5), ('f', 6), ('f', 7), ('y', 1, 0, 4), ('t', 1),
    ('y', 0, 0, 3), ('y', 1, 0, 3), ('y', 0, 1, 3), ('c', 14), ('c', 17), ('z', 14, 0), ('z', 17, 0), ('x', 4),
    ('peer',), ('y', 1, 1, 3), ('z', 14, 1), ('z', 17, 1), ('z', 14, 2), ('z', 17, 2), ('c', 8), ('c', 13),
    ('z', 14, 3), ('z', 17, 3), ('c', 16), ('c', 19), ('z', 8, 0), ('z', 13, 0), ('z', 16, 0), ('c', 22),
    ('z', 19, 0), ('c', 25), ('z', 8, 1), ('z', 13, 1), ('z', 16, 1), ('z', 22, 0), ('z', 19, 1), ('z', 25, 0),
    ('c', 26), ('z', 8, 2), ('z', 13, 2), ('y', 1, 1, 4), ('f', 14), ('f', 17), ('z', 16, 2), ('z', 22, 1),
    ('c', 10), ('z', 19, 2), ('c', 12), ('z', 25, 1), ('z', 26, 0), ('c', 20), ('z', 8, 3), ('z', 13, 3),
    ('c', 24), ('z', 16, 3), ('z', 22, 2), ('z', 10, 0), ('z', 12, 0), ('z', 19, 3), ('z', 25, 2), ('z', 20, 0),
    ('z', 26, 1), ('z', 24, 0), ('f', 8), ('c', 9), ('f', 13), ('z', 22, 3), ('f', 16), ('z', 10, 1),
    ('z', 12, 1), ('f', 19), ('z', 25, 3), ('z', 9, 0), ('z', 20, 1), ('c', 11), ('z', 24, 1), ('z', 26, 2),
    ('c', 15), ('c', 21), ('z', 10, 2), ('z', 12, 2), ('f', 22), ('c', 18), ('z', 9, 1), ('c', 23),
    ('z', 11, 0), ('c', 27), ('z', 15, 0), ('z', 20, 2), ('z', 21, 0), ('z', 24, 2), ('z', 26, 3), ('f', 25),
    ('z', 10, 3), ('z', 12, 3), ('z', 18, 0), ('z', 23, 0), ('z', 9, 2), ('z', 27, 0), ('z', 11, 1), ('z', 15, 1),
    ('z', 20, 3), ('z', 21, 1), ('z', 24, 3), ('f', 26), ('f', 10), ('own',), ('f', 12), ('z', 18, 1),
    ('z', 23, 1), ('z', 9, 3), ('z', 27, 1), ('z', 11, 2), ('z', 15, 2), ('f', 20), ('z', 21, 2), ('f', 24),
    ('z', 18, 2), ('z', 23, 2), ('f', 9), ('z', 27, 2), ('z', 11, 3), ('z', 15, 3), ('z', 21, 3), ('z', 18, 3),
    ('z', 23, 3), ('z', 27, 3), ('u',), ('m', 0, 0), ('m', 0, 1), ('f', 11), ('f', 15), ('f', 21),
    ('f', 18), ('m', 1, 1), ('f', 23), ('f', 27), ('self',), ('m', 2, 1), ('m', 2, 0), ('m', 1, 0),
    ('far',), ('next',),
)


def kernel(scale, given_ref, out_ref, a_ref, G, Q, QP, RL, T, CR, ZR, R, PR, D, O1, O2, MB, MT, MO, DU, MTU, MOU,
           xs, xr, ys, yr, cs, cr, zs, zr, ds, dr, ms, mr, ts, tr, os):
    col, tok = lax.axis_index("col"), lax.axis_index("tok")
    lo, y = col // 4, col % 4
    z, hi, c = tok // 4, (tok // 2) % 2, tok % 2
    x = 2 * hi + lo
    s = y // 2

    def at(x_, y_, z_, c_):
        return ((x_ % 2) * 4 + y_, z_ * 4 + (x_ // 2) * 2 + c_)

    x_next, x_prev, x_opposite = (x + 1) % 4, (x + 3) % 4, (x + 2) % 4
    y_next, y_prev, y_far = (y + 1) % 4, (y + 3) % 4, (y + 2) % 4
    x_dev = (at(x_next, y, z, c), at(x_prev, y, z, c))
    x_from = (x_prev, x_next)
    y_up, y_down = at(x, y_next, z, c), at(x, y_prev, z, c)
    sibling = at(x, y, z, 1 - c)
    z_dev = (at(x, y, (z + 1) % 8, c), at(x, y, (z + 7) % 8, c))
    far_lo = (lo + s) % 2
    half_lo = {"p": lo, "r": lo, "0": 1 - lo, "1": 1 - lo, "f": far_lo, "g": far_lo, "u": 1 - lo}
    half_h = {"p": hi, "r": 1 - hi, "0": 0, "1": 1, "f": hi, "g": 1 - hi, "u": x_next // 2}

    def send(src, dst, s_sem, r_sem, dev):
        cp = pltpu.make_async_remote_copy(src_ref=src, dst_ref=dst, send_sem=s_sem, recv_sem=r_sem,
                                          device_id=dev, device_id_type=MESH)
        cp.start()

    def taken(ref, sem):
        pltpu.make_async_copy(ref, ref, sem).wait()

    partners = [at(2 * (hi ^ dh) + (lo ^ dl), y, z, c ^ dc)
                for dh in range(2) for dl in range(2) for dc in range(2) if dh + dl + dc]
    partners += [at(x, y, (z + dz) % 8, c) for dz in range(1, 8)]
    partners += [at(x, (y + dy) % 4, z, c) for dy in range(1, 4)]
    barrier = pltpu.get_barrier_semaphore()
    for dev in partners:
        pl.semaphore_signal(barrier, inc=1, device_id=dev, device_id_type=MESH)
    given = pltpu.make_async_copy(given_ref, a_ref, os.at[0])
    given.start()

    def reorder(h, part):
        p = lax.broadcasted_iota(jnp.int32, (BLOCK, HALF), 1)
        f = lax.broadcasted_iota(jnp.int32, (BLOCK, HALF), 0)
        feature = ((p // PART) % 8) * 128 + h * 64 + ((p // 128) % 2) * 32 + (p // CH) * PART + p % PART
        pick = (f == feature).astype(F32).astype(BF16)
        rows = pl.ds(part * HALF, HALF)
        v = jnp.dot(a_ref[rows, :], pick, preferred_element_type=F32).astype(BF16)
        for cc in (A, B):
            G[x, h, cc, rows, :] = v[:, cc * CH:cc * CH + CH]

    def turn(x_, h, cc, dst):
        r = lax.broadcasted_iota(jnp.int32, (CH, CH), 0)
        f = lax.broadcasted_iota(jnp.int32, (CH, CH), 1)
        one = (r == f).astype(F32).astype(BF16)
        dst[...] = lax.dot_general(one, G[x_, h, cc], LAST, preferred_element_type=F32).astype(BF16)

    def h_of(x_):
        return x_ // 2

    def x_sent(n, d):
        b = x_from[d]
        return {0: (x, 1 - hi, A, d), 1: (b, 1 - h_of(b), A, d), 2: (x, 1 - hi, B, d), 3: (b, 1 - h_of(b), B, d),
                4: (x, hi, A, d), 5: (x, 0, A, 1 - d), 6: (x, 1, A, 1 - d), 7: (b, h_of(b), A, d),
                8: (x, hi, B, d), 9: (x, 0, B, 1 - d), 10: (x, 1, B, 1 - d), 11: (b, h_of(b), B, d)}[n]

    def x_unit(x_, h, cc, part):
        return G.at[x_, h, cc, pl.ds(part * HALF, HALF), :]

    def x_send(*messages):
        for n in messages:
            for d in range(2):
                u = x_unit(*x_sent(n, d))
                send(u, u, xs.at[0], xr.at[n], x_dev[d])

    low, high = pl.ds(0, W), pl.ds(W, CH - W)
    slots = (hi, 1 - hi)

    def y_landing(k, r, m):
        q = slots[k]
        return (Q.at[1, q, r, low], Q.at[1, q, r, high], RL.at[2 * k + r], Q.at[2, q, r, low], Q.at[2, q, r, high])[m]

    def y_send(k, r, *messages):
        for m in messages:
            q = slots[k]
            src = (Q.at[0, q, r, low], Q.at[0, q, r, high], Q.at[0, q, r, high], Q.at[1, q, r, low], RL.at[2 * k + r])[m]
            send(src, y_landing(k, r, m), ys.at[m], yr.at[2 * k + r, m], y_down if m in (0, 1, 3) else y_up)

    waited = set()

    def need_x(*messages):
        for n in messages:
            if ("x", n) not in waited:
                waited.add(("x", n))
                taken(G.at[0, 0, 0], xr.at[n])

    def need_y(k, r, *messages):
        for m in messages:
            if ("y", k, r, m) not in waited:
                waited.add(("y", k, r, m))
                taken(y_landing(k, r, m), yr.at[2 * k + r, m])

    def x_step(n):
        if n:
            need_x(X_FORWARD[X_GROUPS[n][0]])
        x_send(*X_GROUPS[n])

    def q_step(r):
        need_x((1, 3)[r])
        turn(x_opposite, hi, r, Q.at[0, 1 - hi, r])
        y_send(1, r, 0, 2, 1)
        if r == A and not OWN_FIRST:
            y_send(0, B, 0, 2, 1)

    def y_step(k, r, m):
        need_y(k, r, 0 if m == 3 else 2)
        y_send(k, r, m)

    def compute(cell):
        for j, (kind, r, half, cc) in enumerate(CELLS[cell]):
            l, h = half_lo[half], half_h[half]
            if kind in (OWN, PEER):
                rows = QP[r] if kind == PEER else Q[0, hi, r]
                acc = jnp.dot(rows, G[x, h, cc], preferred_element_type=F32)
            else:
                need_x(*X_NEEDS[half, cc])
                for k in range(2):
                    need_y(k, r, *((), (0, 1), (3, 4))[kind - SELF])
                acc = jnp.dot(Q[kind - SELF, 0, r], G[l, h, cc], preferred_element_type=F32)
                acc += jnp.dot(Q[kind - SELF, 1, r], G[2 + l, h, cc], preferred_element_type=F32)
            T[cell, :, :, :, j * CH:j * CH + CH] = acc.reshape(2, 8, PART, CH)
        w = width(cell)
        send(T.at[cell, 1 - c, :, :, w], CR.at[cell, :, :, w], cs.at[0], cr.at[cell], sibling)

    def width(cell):
        return pl.ds(0, CH * len(CELLS[cell]))

    def z_landed(cell, step):
        w = width(cell)
        taken(ZR.at[cell, :, step, :, w] if step else ZR.at[cell, 0, 0, :, w], zr.at[cell, step])

    def z_step(cell, step):
        w, n = width(cell), CH * len(CELLS[cell]) // 2
        sides = (pl.ds(0, n), pl.ds(n, n))
        if step == 0:
            taken(CR.at[cell, :, :, w], cr.at[cell])
        else:
            z_landed(cell, step - 1)
        for d in range(2):
            to = (z + 4 - step) % 8 if d == 0 else (z + 4 + step) % 8
            if step == 0:
                cols = sides[d]
                T[cell, c, to, :, cols] = T[cell, c, to, :, cols] + CR[cell, to, :, cols]
                send(T.at[cell, c, to, :, cols], ZR.at[cell, d, 0, :, cols], zs.at[0], zr.at[cell, 0], z_dev[d])
                continue
            if step == 1:
                cols, rest = sides[d], sides[1 - d]
                T[cell, c, to, :, cols] = T[cell, c, to, :, cols] + CR[cell, to, :, cols] + ZR[cell, d, 0, :, cols]
                T[cell, c, to, :, rest] = T[cell, c, to, :, rest] + CR[cell, to, :, rest]
            else:
                T[cell, c, to, :, w] = T[cell, c, to, :, w] + CR[cell, to, :, w] + ZR[cell, d, step - 1, :, w]
            send(T.at[cell, c, to, :, w], ZR.at[cell, d, step, :, w], zs.at[0], zr.at[cell, step], z_dev[d])

    def out_cols(l, y_):
        return pl.ds(pl.multiple_of((l * 4 + y_) * BLOCK, BLOCK), BLOCK)

    def group(j, k):
        return pl.ds(pl.multiple_of(j * CH + k * 128, 128), 128)

    def mirror_self(half, k):
        return "no" if k else {"p": "yes", "f": "some"}.get(half, "no")

    def finish(cell):
        z_landed(cell, 3)
        w = width(cell)
        R[cell, :, w] = T[cell, c, z, :, w] + CR[cell, z, :, w] + ZR[cell, 0, 3, :, w] + ZR[cell, 1, 3, :, w]
        for j, (kind, r, half, cc) in enumerate(CELLS[cell]):
            l, h = half_lo[half], half_h[half]
            cols = pl.ds(j * CH, CH)
            src = R.at[cell, :, cols]
            if kind == OWN:
                D[h, cc, r] = R[cell, :, cols]
                continue
            if kind == SELF:
                DU[cc, r] = R[cell, :, cols]
                for k in range(2):
                    send(R.at[cell, :, pl.ds(j * CH + k * 128, 128)], MB.at[cc, 12 + c, r], ms.at[2], mr.at[3, 0],
                         at(x_next, y, z, k))
                continue
            if kind == PEER:
                continue
            if kind == NEXT:
                send(src, O1.at[l, h, cc, r], ds.at[1], dr.at[1], y_up)
            else:
                send(src, O2.at[h, cc, r], ds.at[2], dr.at[2], at(x, y_far, z, c))
            mine = (8 if kind == FAR else lo * 4) + hi * 2 + c
            s_sem, batch = ms.at[kind - NEXT], 2 if kind == FAR else 1 if half in "pr" else 0
            for dk in range(2):
                k = (c + dk) % 2
                part, dst, dev = R.at[cell, :, group(j, k)], MB.at[cc, mine, r], at(2 * h + l, y, z, k)
                stays = mirror_self(half, dk)

                def leave():
                    send(part, dst, s_sem, mr.at[batch, cc], dev)

                def keep():
                    MB[cc, mine, r] = R[cell, :, group(j, k)]
                if stays == "no":
                    leave()
                elif stays == "yes":
                    keep()
                else:
                    pl.when(s == 0)(keep)
                    pl.when(s == 1)(leave)

    def send_peer():
        for cell, tiles in enumerate(CELLS):
            for j, (kind, r, half, cc) in enumerate(tiles):
                if kind == PEER:
                    send(R.at[cell, :, pl.ds(j * CH, CH)], PR.at[half_h[half], cc, r], ds.at[0], dr.at[0], at(x_opposite, y, z, c))

    mirror_base = ((1 - lo) * 4, lo * 4, 8)

    def mirror(b, cc):
        def take(n):
            taken(MB.at[cc, 0:n], mr.at[b, cc])
        if b < 2:
            take(4 - b)
        else:
            pl.when(s == 0)(lambda: take(3))
            pl.when(s == 1)(lambda: take(4))
        turned = jnp.transpose(MB[cc, pl.ds(mirror_base[b], 4)].reshape(4 * ROWS, 4 * ROWS))
        MT[b, cc] = turned.reshape(8, PART, 4 * ROWS) * scale
        MO[b, z, cc] = MT[b, cc, z]
        for dz in range(1, 8):
            to = (z + dz) % 8
            send(MT.at[b, cc, to], MO.at[b, z, cc], ts.at[0], tr.at[b, cc], at(x, y, to, c))

    def mirror_next_x():
        taken(MB.at[0, 0:4], mr.at[3, 0])
        turned = [jnp.transpose(MB[cc, 12:14].reshape(2 * ROWS, 4 * ROWS)).reshape(8, PART, 2 * ROWS) for cc in (A, B)]
        MTU[...] = jnp.concatenate(turned, axis=2) * scale
        MOU[z] = MTU[z]
        for dz in range(1, 8):
            to = (z + dz) % 8
            send(MTU.at[to], MOU.at[z], ts.at[1], tr.at[3, 0], at(x, y, to, c))

    def store(l, y_, v):
        out_ref[:, out_cols(l, y_)] = v

    def natural(v):
        t = [[v[h, cc].reshape(ROWS, CH) for cc in (A, B)] for h in range(2)]
        return scale * jnp.concatenate([t[h][cc][:, k * 128 + b * PART:k * 128 + b * PART + PART]
                                        for b in range(8) for h in range(2) for k in range(2) for cc in (A, B)], axis=1)

    def store_mirror(b, l, y_):
        for cc in (A, B):
            taken(MO.at[b, 0:7, cc], tr.at[b, cc])
        store(l, y_, jnp.concatenate([MO[b, k].reshape(ROWS, 4 * ROWS) for k in range(8)], axis=1))

    def store_own():
        taken(PR, dr.at[0])
        store(lo, y, natural(D[...] + PR[...]))

    def store_next():
        taken(O1, dr.at[1])
        for l in range(2):
            store(l, y_prev, natural(O1[l]))

    def store_far():
        taken(O2, dr.at[2])
        store((lo + 1 - s) % 2, y_far, natural(O2[...]))

    def store_self():
        taken(MOU.at[0:7], tr.at[3, 0])
        direct = [DU[cc].reshape(ROWS, CH) * scale for cc in (A, B)]
        first = x_next // 2 == 0
        groups = []
        for b in range(8):
            own = jnp.concatenate([direct[cc][:, k * 128 + b * PART:k * 128 + b * PART + PART]
                                   for k in range(2) for cc in (A, B)], axis=1)
            other = jnp.concatenate([MOU[b, :, cc * 64:cc * 64 + 64] for cc in (A, B)], axis=0)
            groups += [jnp.where(first, own, other), jnp.where(first, other, own)]
        store(1 - lo, y, jnp.concatenate(groups, axis=1))

    given.wait()
    for part in range(2):
        reorder(1 - hi, part)
    pl.semaphore_wait(barrier, len(partners))
    x_step(0)
    for part in range(2):
        reorder(hi, part)
    turn(x, hi, A, Q.at[0, hi, A])
    y_send(0, A, 0, 2, 1)
    turn(x, hi, B, Q.at[0, hi, B])
    if OWN_FIRST:
        y_send(0, B, 0, 2, 1)
    for cc in (A, B):
        turn(x, 1 - hi, cc, QP.at[cc])

    steps = {"x": x_step, "t": q_step, "u": mirror_next_x, "y": y_step, "c": compute, "z": z_step, "f": finish, "m": mirror, "peer": send_peer, "own": store_own, "next": store_next,
             "far": store_far, "self": store_self}
    for name, *which in ORDER:
        steps[name](*which)
    store_mirror(0, 1 - lo, y_next)
    store_mirror(1, lo, y_next)
    store_mirror(2, far_lo, y_far)

    taken(G.at[0:3], xs.at[0])
    for m in range(5):
        taken(Q.at[0, :, :, low if m in (0, 3) else high], ys.at[m])
    taken(CR.at[0:PAIRS], cs.at[0])
    taken(CR.at[0:PAIRS, 0:7], zs.at[0])
    for n, ref in enumerate((PR, O1, O2)):
        taken(ref, ds.at[n])
    taken(MB.at[:, 0:7], ms.at[0])
    for v in range(2):
        pl.when(s == v)(lambda: taken(MB.at[:, 0:3 + v], ms.at[1]))
    taken(MB.at[0, 0:4], ms.at[2])
    taken(MT.at[:, :, 0:7], ts.at[0])
    taken(MTU.at[0:7], ts.at[1])


def solution(mesh):
    token_ranks = mesh.shape["tok"]

    def shards(activations):
        scale = 1.0 / (activations.shape[0] * token_ranks)
        dma = pltpu.SemaphoreType.DMA
        return pl.pallas_call(
            lambda *refs: kernel(scale, *refs),
            out_shape=pltpu.VMEM((ROWS, 8 * BLOCK), F32),
            in_specs=[pl.BlockSpec(memory_space=pl.ANY)],
            out_specs=pl.BlockSpec(memory_space=pltpu.VMEM),
            scratch_shapes=[
                pltpu.VMEM((BLOCK, BLOCK), BF16),
                pltpu.VMEM((4, 2, 2, BLOCK, CH), BF16),
                pltpu.VMEM((3, 2, 2, CH, BLOCK), BF16),
                pltpu.VMEM((2, CH, BLOCK), BF16),
                pltpu.VMEM((4, CH - W, BLOCK), BF16),
                pltpu.VMEM((COUNT, 2, 8, PART, HALF), F32),
                pltpu.VMEM((COUNT, 8, PART, HALF), F32),
                pltpu.VMEM((COUNT, 2, 4, PART, HALF), F32),
                pltpu.VMEM((COUNT, PART, HALF), F32),
                pltpu.VMEM((2, 2, 2, PART, CH), F32),
                pltpu.VMEM((2, 2, 2, PART, CH), F32),
                pltpu.VMEM((2, 2, 2, 2, PART, CH), F32),
                pltpu.VMEM((2, 2, 2, PART, CH), F32),
                pltpu.VMEM((2, 14, 2, PART, 4 * ROWS), F32),
                pltpu.VMEM((3, 2, 8, PART, 4 * ROWS), F32),
                pltpu.VMEM((3, 8, 2, PART, 4 * ROWS), F32),
                pltpu.VMEM((2, 2, PART, CH), F32),
                pltpu.VMEM((8, PART, 4 * ROWS), F32),
                pltpu.VMEM((8, PART, 4 * ROWS), F32),
                dma((1,)), dma((12,)),
                dma((5,)), dma((4, 5)),
                dma((1,)), dma((COUNT,)),
                dma((1,)), dma((COUNT, 4)),
                dma((3,)), dma((3,)),
                dma((3,)), dma((4, 2)),
                dma((2,)), dma((4, 2)),
                dma((1,)),
            ],
            compiler_params=pltpu.CompilerParams(
                collective_id=0, has_side_effects=True, vmem_limit_bytes=56 * 1024 * 1024),
            cost_estimate=pl.CostEstimate(flops=14 * 10**9, bytes_accessed=3 * 2**20, transcendentals=0),
            name="gram",
        )(activations)

    return jax.shard_map(shards, mesh=mesh, in_specs=(P("tok", "col"),), out_specs=P(("col", "tok"), None), check_vma=False)
```

```python
import jax
import jax.numpy as jnp
from jax import lax
from jax.experimental import pallas as pl
from jax.experimental.pallas import tpu as pltpu
from jax.sharding import PartitionSpec as P

MESH = pl.DeviceIdType.MESH
F32, BF16 = jnp.float32, jnp.bfloat16
BLOCK = 1024
HALF = BLOCK // 2
CH = HALF // 2
ROWS = 32
PART = ROWS // 2
W = 80
LAST = (((1,), (1,)), ((), ()))
A, B = 0, 1
OWN, PEER, SELF, NEXT, FAR = range(5)
CELLS = (
    ((OWN, A, "p", A), (OWN, A, "p", B),),
    ((OWN, A, "r", A), (OWN, A, "r", B),),
    ((OWN, B, "p", A), (OWN, B, "p", B),),
    ((OWN, B, "r", A), (OWN, B, "r", B),),
    ((PEER, A, "p", A), (PEER, A, "p", B),),
    ((PEER, A, "r", A), (PEER, A, "r", B),),
    ((PEER, B, "p", A), (PEER, B, "p", B),),
    ((PEER, B, "r", A), (PEER, B, "r", B),),
    ((NEXT, A, "0", A), (SELF, B, "u", A),),
    ((NEXT, A, "r", B), (NEXT, B, "r", B),),
    ((FAR, A, "f", B), (NEXT, B, "0", B),),
    ((FAR, A, "g", B), (FAR, B, "g", B),),
    ((SELF, A, "u", B),),
    ((NEXT, A, "1", A),),
    ((NEXT, A, "p", A),),
    ((FAR, B, "f", B),),
    ((NEXT, B, "p", A),),
    ((NEXT, A, "p", B),),
    ((NEXT, B, "r", A), (FAR, B, "g", A),),
    ((NEXT, B, "p", B), (SELF, A, "u", A),),
    ((NEXT, B, "0", A), (SELF, B, "u", B),),
    ((FAR, B, "f", A),),
    ((NEXT, B, "1", B),),
    ((FAR, A, "g", A),),
    ((NEXT, A, "0", B),),
    ((NEXT, A, "1", B), (NEXT, B, "1", A),),
    ((FAR, A, "f", A),),
    ((NEXT, A, "r", A),),
)
COUNT = len(CELLS)
PAIRS = sum(len(tiles) for tiles in CELLS) // 2
X_NEEDS = {("p", A): (1,), ("p", B): (3,), ("r", A): (7,), ("r", B): (11,), ("0", A): (0, 4, 5), ("0", B): (2, 8, 9),
           ("1", A): (0, 4, 6), ("1", B): (2, 8, 10), ("f", A): (1, 0, 4, 5, 6), ("f", B): (3, 2, 8, 9, 10),
           ("g", A): (7, 0, 4, 5, 6), ("g", B): (11, 2, 8, 9, 10), ("u", A): (0, 4, 5, 6), ("u", B): (2, 8, 9, 10)}
X_FORWARD = {1: 0, 3: 2, 7: 4, 11: 8}
X_GROUPS = ((0, 2), (1, 8, 5), (3, 4, 6, 10, 9), (11,), (7,))
OWN_FIRST = True

ORDER = (
    ('c', 0), ('c', 1), ('c', 2), ('c', 3), ('c', 4), ('c', 5), ('c', 6), ('z', 0, 0),
    ('c', 7), ('z', 1, 0), ('z', 2, 0), ('x', 1), ('z', 3, 0), ('z', 4, 0), ('z', 5, 0), ('z', 6, 0),
    ('z', 0, 1), ('z', 7, 0), ('z', 1, 1), ('z', 2, 1), ('z', 3, 1), ('z', 4, 1), ('z', 5, 1), ('y', 0, 0, 4),
    ('z', 6, 1), ('z', 0, 2), ('z', 7, 1), ('x', 2), ('z', 1, 2), ('z', 2, 2), ('z', 3, 2), ('z', 4, 2),
    ('z', 5, 2), ('z', 6, 2), ('z', 0, 3), ('z', 7, 2), ('t', 0), ('y', 0, 1, 4), ('z', 1, 3), ('z', 2, 3),
    ('z', 3, 3), ('z', 4, 3), ('z', 5, 3), ('z', 6, 3), ('f', 0), ('z', 7, 3), ('x', 3), ('f', 1),
    ('f', 2), ('f', 3), ('f', 4), ('f', 5), ('f', 6), ('f', 7), ('y', 1, 0, 4), ('t', 1),
    ('y', 0, 0, 3), ('y', 1, 0, 3), ('y', 0, 1, 3), ('c', 14), ('c', 17), ('z', 14, 0), ('z', 17, 0), ('x', 4),
    ('peer',), ('y', 1, 1, 3), ('z', 14, 1), ('z', 17, 1), ('z', 14, 2), ('z', 17, 2), ('c', 8), ('c', 13),
    ('z', 14, 3), ('z', 17, 3), ('c', 16), ('c', 19), ('z', 8, 0), ('z', 13, 0), ('z', 16, 0), ('c', 22),
    ('z', 19, 0), ('c', 25), ('z', 8, 1), ('z', 13, 1), ('z', 16, 1), ('z', 22, 0), ('z', 19, 1), ('z', 25, 0),
    ('c', 26), ('z', 8, 2), ('z', 13, 2), ('y', 1, 1, 4), ('f', 14), ('f', 17), ('z', 16, 2), ('z', 22, 1),
    ('c', 10), ('z', 19, 2), ('c', 12), ('z', 25, 1), ('z', 26, 0), ('c', 20), ('z', 8, 3), ('z', 13, 3),
    ('c', 24), ('z', 16, 3), ('z', 22, 2), ('z', 10, 0), ('z', 12, 0), ('z', 19, 3), ('z', 25, 2), ('z', 20, 0),
    ('z', 26, 1), ('z', 24, 0), ('f', 8), ('c', 9), ('f', 13), ('z', 22, 3), ('f', 16), ('z', 10, 1),
    ('z', 12, 1), ('f', 19), ('z', 25, 3), ('z', 9, 0), ('z', 20, 1), ('z', 24, 1), ('z', 26, 2), ('c', 11),
    ('c', 15), ('z', 10, 2), ('z', 12, 2), ('c', 21), ('z', 20, 2), ('z', 9, 1), ('c', 18), ('z', 24, 2),
    ('z', 26, 3), ('z', 11, 0), ('c', 23), ('z', 15, 0), ('f', 22), ('c', 27), ('z', 21, 0), ('f', 25),
    ('z', 10, 3), ('z', 12, 3), ('z', 18, 0), ('z', 23, 0), ('z', 9, 2), ('z', 27, 0), ('z', 11, 1), ('z', 15, 1),
    ('z', 20, 3), ('z', 21, 1), ('z', 24, 3), ('f', 26), ('f', 10), ('own',), ('f', 12), ('z', 18, 1),
    ('z', 23, 1), ('z', 9, 3), ('z', 27, 1), ('z', 11, 2), ('z', 15, 2), ('f', 20), ('z', 21, 2), ('f', 24),
    ('z', 18, 2), ('z', 23, 2), ('f', 9), ('z', 27, 2), ('z', 11, 3), ('z', 15, 3), ('z', 21, 3), ('z', 18, 3),
    ('z', 23, 3), ('z', 27, 3), ('u',), ('m', 0, 0), ('m', 0, 1), ('f', 11), ('f', 15), ('f', 21),
    ('f', 18), ('m', 1, 1), ('f', 23), ('f', 27), ('m', 2, 1), ('m', 2, 0), ('m', 1, 0), ('next',),
    ('self',), ('far',),
)


def kernel(scale, given_ref, out_ref, a_ref, G, Q, QP, RL, T, CR, ZR, R, PR, D, O1, O2, MB, MT, MO, DU, MTU, MOU,
           xs, xr, ys, yr, cs, cr, zs, zr, ds, dr, ms, mr, ts, tr, os):
    col, tok = lax.axis_index("col"), lax.axis_index("tok")
    lo, y = col // 4, col % 4
    z, hi, c = tok // 4, (tok // 2) % 2, tok % 2
    x = 2 * hi + lo
    s = y // 2

    def at(x_, y_, z_, c_):
        return ((x_ % 2) * 4 + y_, z_ * 4 + (x_ // 2) * 2 + c_)

    x_next, x_prev, x_opposite = (x + 1) % 4, (x + 3) % 4, (x + 2) % 4
    y_next, y_prev, y_far = (y + 1) % 4, (y + 3) % 4, (y + 2) % 4
    x_dev = (at(x_next, y, z, c), at(x_prev, y, z, c))
    x_from = (x_prev, x_next)
    y_up, y_down = at(x, y_next, z, c), at(x, y_prev, z, c)
    sibling = at(x, y, z, 1 - c)
    z_dev = (at(x, y, (z + 1) % 8, c), at(x, y, (z + 7) % 8, c))
    far_lo = (lo + s) % 2
    half_lo = {"p": lo, "r": lo, "0": 1 - lo, "1": 1 - lo, "f": far_lo, "g": far_lo, "u": 1 - lo}
    half_h = {"p": hi, "r": 1 - hi, "0": 0, "1": 1, "f": hi, "g": 1 - hi, "u": x_next // 2}

    def send(src, dst, s_sem, r_sem, dev):
        cp = pltpu.make_async_remote_copy(src_ref=src, dst_ref=dst, send_sem=s_sem, recv_sem=r_sem,
                                          device_id=dev, device_id_type=MESH)
        cp.start()

    def taken(ref, sem):
        pltpu.make_async_copy(ref, ref, sem).wait()

    partners = [at(2 * (hi ^ dh) + (lo ^ dl), y, z, c ^ dc)
                for dh in range(2) for dl in range(2) for dc in range(2) if dh + dl + dc]
    partners += [at(x, y, (z + dz) % 8, c) for dz in range(1, 8)]
    partners += [at(x, (y + dy) % 4, z, c) for dy in range(1, 4)]
    barrier = pltpu.get_barrier_semaphore()
    for dev in partners:
        pl.semaphore_signal(barrier, inc=1, device_id=dev, device_id_type=MESH)
    given = pltpu.make_async_copy(given_ref, a_ref, os.at[0])
    given.start()

    def reorder(h, part):
        p = lax.broadcasted_iota(jnp.int32, (BLOCK, HALF), 1)
        f = lax.broadcasted_iota(jnp.int32, (BLOCK, HALF), 0)
        feature = ((p // PART) % 8) * 128 + h * 64 + ((p // 128) % 2) * 32 + (p // CH) * PART + p % PART
        pick = (f == feature).astype(F32).astype(BF16)
        rows = pl.ds(part * HALF, HALF)
        v = jnp.dot(a_ref[rows, :], pick, preferred_element_type=F32).astype(BF16)
        for cc in (A, B):
            G[x, h, cc, rows, :] = v[:, cc * CH:cc * CH + CH]

    def turn(x_, h, cc, dst):
        r = lax.broadcasted_iota(jnp.int32, (CH, CH), 0)
        f = lax.broadcasted_iota(jnp.int32, (CH, CH), 1)
        one = (r == f).astype(F32).astype(BF16)
        dst[...] = lax.dot_general(one, G[x_, h, cc], LAST, preferred_element_type=F32).astype(BF16)

    def h_of(x_):
        return x_ // 2

    def x_sent(n, d):
        b = x_from[d]
        return {0: (x, 1 - hi, A, d), 1: (b, 1 - h_of(b), A, d), 2: (x, 1 - hi, B, d), 3: (b, 1 - h_of(b), B, d),
                4: (x, hi, A, d), 5: (x, 0, A, 1 - d), 6: (x, 1, A, 1 - d), 7: (b, h_of(b), A, d),
                8: (x, hi, B, d), 9: (x, 0, B, 1 - d), 10: (x, 1, B, 1 - d), 11: (b, h_of(b), B, d)}[n]

    def x_unit(x_, h, cc, part):
        return G.at[x_, h, cc, pl.ds(part * HALF, HALF), :]

    def x_send(*messages):
        for n in messages:
            for d in range(2):
                u = x_unit(*x_sent(n, d))
                send(u, u, xs.at[0], xr.at[n], x_dev[d])

    low, high = pl.ds(0, W), pl.ds(W, CH - W)
    slots = (hi, 1 - hi)

    def y_landing(k, r, m):
        q = slots[k]
        return (Q.at[1, q, r, low], Q.at[1, q, r, high], RL.at[2 * k + r], Q.at[2, q, r, low], Q.at[2, q, r, high])[m]

    def y_send(k, r, *messages):
        for m in messages:
            q = slots[k]
            src = (Q.at[0, q, r, low], Q.at[0, q, r, high], Q.at[0, q, r, high], Q.at[1, q, r, low], RL.at[2 * k + r])[m]
            send(src, y_landing(k, r, m), ys.at[m], yr.at[2 * k + r, m], y_down if m in (0, 1, 3) else y_up)

    waited = set()

    def need_x(*messages):
        for n in messages:
            if ("x", n) not in waited:
                waited.add(("x", n))
                taken(G.at[0, 0, 0], xr.at[n])

    def need_y(k, r, *messages):
        for m in messages:
            if ("y", k, r, m) not in waited:
                waited.add(("y", k, r, m))
                taken(y_landing(k, r, m), yr.at[2 * k + r, m])

    def x_step(n):
        if n:
            need_x(X_FORWARD[X_GROUPS[n][0]])
        x_send(*X_GROUPS[n])

    def q_step(r):
        need_x((1, 3)[r])
        turn(x_opposite, hi, r, Q.at[0, 1 - hi, r])
        y_send(1, r, 0, 2, 1)
        if r == A and not OWN_FIRST:
            y_send(0, B, 0, 2, 1)

    def y_step(k, r, m):
        need_y(k, r, 0 if m == 3 else 2)
        y_send(k, r, m)

    def compute(cell):
        for j, (kind, r, half, cc) in enumerate(CELLS[cell]):
            l, h = half_lo[half], half_h[half]
            if kind in (OWN, PEER):
                rows = QP[r] if kind == PEER else Q[0, hi, r]
                acc = jnp.dot(rows, G[x, h, cc], preferred_element_type=F32)
            else:
                need_x(*X_NEEDS[half, cc])
                for k in range(2):
                    need_y(k, r, *((), (0, 1), (3, 4))[kind - SELF])
                acc = jnp.dot(Q[kind - SELF, 0, r], G[l, h, cc], preferred_element_type=F32)
                acc += jnp.dot(Q[kind - SELF, 1, r], G[2 + l, h, cc], preferred_element_type=F32)
            T[cell, :, :, :, j * CH:j * CH + CH] = acc.reshape(2, 8, PART, CH)
        w = width(cell)
        send(T.at[cell, 1 - c, :, :, w], CR.at[cell, :, :, w], cs.at[0], cr.at[cell], sibling)

    def width(cell):
        return pl.ds(0, CH * len(CELLS[cell]))

    def z_landed(cell, step):
        w = width(cell)
        taken(ZR.at[cell, :, step, :, w] if step else ZR.at[cell, 0, 0, :, w], zr.at[cell, step])

    def z_step(cell, step):
        w, n = width(cell), CH * len(CELLS[cell]) // 2
        sides = (pl.ds(0, n), pl.ds(n, n))
        if step == 0:
            taken(CR.at[cell, :, :, w], cr.at[cell])
        else:
            z_landed(cell, step - 1)
        for d in range(2):
            to = (z + 4 - step) % 8 if d == 0 else (z + 4 + step) % 8
            if step == 0:
                cols = sides[d]
                T[cell, c, to, :, cols] = T[cell, c, to, :, cols] + CR[cell, to, :, cols]
                send(T.at[cell, c, to, :, cols], ZR.at[cell, d, 0, :, cols], zs.at[0], zr.at[cell, 0], z_dev[d])
                continue
            if step == 1:
                cols, rest = sides[d], sides[1 - d]
                T[cell, c, to, :, cols] = T[cell, c, to, :, cols] + CR[cell, to, :, cols] + ZR[cell, d, 0, :, cols]
                T[cell, c, to, :, rest] = T[cell, c, to, :, rest] + CR[cell, to, :, rest]
            else:
                T[cell, c, to, :, w] = T[cell, c, to, :, w] + CR[cell, to, :, w] + ZR[cell, d, step - 1, :, w]
            send(T.at[cell, c, to, :, w], ZR.at[cell, d, step, :, w], zs.at[0], zr.at[cell, step], z_dev[d])

    def out_cols(l, y_):
        return pl.ds(pl.multiple_of((l * 4 + y_) * BLOCK, BLOCK), BLOCK)

    def group(j, k):
        return pl.ds(pl.multiple_of(j * CH + k * 128, 128), 128)

    def mirror_self(half, k):
        return "no" if k else {"p": "yes", "f": "some"}.get(half, "no")

    def finish(cell):
        z_landed(cell, 3)
        w = width(cell)
        R[cell, :, w] = T[cell, c, z, :, w] + CR[cell, z, :, w] + ZR[cell, 0, 3, :, w] + ZR[cell, 1, 3, :, w]
        for j, (kind, r, half, cc) in enumerate(CELLS[cell]):
            l, h = half_lo[half], half_h[half]
            cols = pl.ds(j * CH, CH)
            src = R.at[cell, :, cols]
            if kind == OWN:
                D[h, cc, r] = R[cell, :, cols]
                continue
            if kind == SELF:
                DU[cc, r] = R[cell, :, cols]
                for k in range(2):
                    send(R.at[cell, :, pl.ds(j * CH + k * 128, 128)], MB.at[cc, 12 + c, r], ms.at[2], mr.at[3, 0],
                         at(x_next, y, z, k))
                continue
            if kind == PEER:
                continue
            mine = (8 if kind == FAR else lo * 4) + hi * 2 + c
            s_sem, batch = ms.at[kind - NEXT], 2 if kind == FAR else 1 if half in "pr" else 0
            for dk in range(2):
                k = (c + dk) % 2
                part, dst, dev = R.at[cell, :, group(j, k)], MB.at[cc, mine, r], at(2 * h + l, y, z, k)
                stays = mirror_self(half, dk)

                def leave():
                    send(part, dst, s_sem, mr.at[batch, cc], dev)

                def keep():
                    MB[cc, mine, r] = R[cell, :, group(j, k)]
                if stays == "no":
                    leave()
                elif stays == "yes":
                    keep()
                else:
                    pl.when(s == 0)(keep)
                    pl.when(s == 1)(leave)
            if kind == NEXT:
                send(src, O1.at[l, h, cc, r], ds.at[1], dr.at[1], y_up)
            else:
                send(src, O2.at[h, cc, r], ds.at[2], dr.at[2], at(x, y_far, z, c))

    def send_peer():
        for cell, tiles in enumerate(CELLS):
            for j, (kind, r, half, cc) in enumerate(tiles):
                if kind == PEER:
                    send(R.at[cell, :, pl.ds(j * CH, CH)], PR.at[half_h[half], cc, r], ds.at[0], dr.at[0], at(x_opposite, y, z, c))

    mirror_base = ((1 - lo) * 4, lo * 4, 8)

    def mirror(b, cc):
        def take(n):
            taken(MB.at[cc, 0:n], mr.at[b, cc])
        if b < 2:
            take(4 - b)
        else:
            pl.when(s == 0)(lambda: take(3))
            pl.when(s == 1)(lambda: take(4))
        turned = jnp.transpose(MB[cc, pl.ds(mirror_base[b], 4)].reshape(4 * ROWS, 4 * ROWS))
        MT[b, cc] = turned.reshape(8, PART, 4 * ROWS) * scale
        MO[b, z, cc] = MT[b, cc, z]
        for dz in range(1, 8):
            to = (z + dz) % 8
            send(MT.at[b, cc, to], MO.at[b, z, cc], ts.at[0], tr.at[b, cc], at(x, y, to, c))

    def mirror_next_x():
        taken(MB.at[0, 0:4], mr.at[3, 0])
        turned = [jnp.transpose(MB[cc, 12:14].reshape(2 * ROWS, 4 * ROWS)).reshape(8, PART, 2 * ROWS) for cc in (A, B)]
        MTU[...] = jnp.concatenate(turned, axis=2) * scale
        MOU[z] = MTU[z]
        for dz in range(1, 8):
            to = (z + dz) % 8
            send(MTU.at[to], MOU.at[z], ts.at[1], tr.at[3, 0], at(x, y, to, c))

    def store(l, y_, v):
        out_ref[:, out_cols(l, y_)] = v

    def natural(v):
        t = [[v[h, cc].reshape(ROWS, CH) for cc in (A, B)] for h in range(2)]
        return scale * jnp.concatenate([t[h][cc][:, k * 128 + b * PART:k * 128 + b * PART + PART]
                                        for b in range(8) for h in range(2) for k in range(2) for cc in (A, B)], axis=1)

    def store_mirror(b, l, y_):
        for cc in (A, B):
            taken(MO.at[b, 0:7, cc], tr.at[b, cc])
        store(l, y_, jnp.concatenate([MO[b, k].reshape(ROWS, 4 * ROWS) for k in range(8)], axis=1))

    def store_own():
        taken(PR, dr.at[0])
        store(lo, y, natural(D[...] + PR[...]))

    def store_next():
        taken(O1, dr.at[1])
        for l in range(2):
            store(l, y_prev, natural(O1[l]))

    def store_far():
        taken(O2, dr.at[2])
        store((lo + 1 - s) % 2, y_far, natural(O2[...]))

    def store_self():
        taken(MOU.at[0:7], tr.at[3, 0])
        direct = [DU[cc].reshape(ROWS, CH) * scale for cc in (A, B)]
        first = x_next // 2 == 0
        groups = []
        for b in range(8):
            own = jnp.concatenate([direct[cc][:, k * 128 + b * PART:k * 128 + b * PART + PART]
                                   for k in range(2) for cc in (A, B)], axis=1)
            other = jnp.concatenate([MOU[b, :, cc * 64:cc * 64 + 64] for cc in (A, B)], axis=0)
            groups += [jnp.where(first, own, other), jnp.where(first, other, own)]
        store(1 - lo, y, jnp.concatenate(groups, axis=1))

    given.wait()
    for part in range(2):
        reorder(1 - hi, part)
    pl.semaphore_wait(barrier, len(partners))
    x_step(0)
    for part in range(2):
        reorder(hi, part)
    turn(x, hi, A, Q.at[0, hi, A])
    y_send(0, A, 0, 2, 1)
    turn(x, hi, B, Q.at[0, hi, B])
    if OWN_FIRST:
        y_send(0, B, 0, 2, 1)
    for cc in (A, B):
        turn(x, 1 - hi, cc, QP.at[cc])

    steps = {"x": x_step, "t": q_step, "u": mirror_next_x, "y": y_step, "c": compute, "z": z_step, "f": finish, "m": mirror, "peer": send_peer, "own": store_own, "next": store_next,
             "far": store_far, "self": store_self}
    for name, *which in ORDER:
        steps[name](*which)
    store_mirror(0, 1 - lo, y_next)
    store_mirror(1, lo, y_next)
    store_mirror(2, far_lo, y_far)

    taken(G.at[0:3], xs.at[0])
    for m in range(5):
        taken(Q.at[0, :, :, low if m in (0, 3) else high], ys.at[m])
    taken(CR.at[0:PAIRS], cs.at[0])
    taken(CR.at[0:PAIRS, 0:7], zs.at[0])
    for n, ref in enumerate((PR, O1, O2)):
        taken(ref, ds.at[n])
    taken(MB.at[:, 0:7], ms.at[0])
    for v in range(2):
        pl.when(s == v)(lambda: taken(MB.at[:, 0:3 + v], ms.at[1]))
    taken(MB.at[0, 0:4], ms.at[2])
    taken(MT.at[:, :, 0:7], ts.at[0])
    taken(MTU.at[0:7], ts.at[1])


def solution(mesh):
    token_ranks = mesh.shape["tok"]

    def shards(activations):
        scale = 1.0 / (activations.shape[0] * token_ranks)
        dma = pltpu.SemaphoreType.DMA
        return pl.pallas_call(
            lambda *refs: kernel(scale, *refs),
            out_shape=pltpu.VMEM((ROWS, 8 * BLOCK), F32),
            in_specs=[pl.BlockSpec(memory_space=pl.ANY)],
            out_specs=pl.BlockSpec(memory_space=pltpu.VMEM),
            scratch_shapes=[
                pltpu.VMEM((BLOCK, BLOCK), BF16),
                pltpu.VMEM((4, 2, 2, BLOCK, CH), BF16),
                pltpu.VMEM((3, 2, 2, CH, BLOCK), BF16),
                pltpu.VMEM((2, CH, BLOCK), BF16),
                pltpu.VMEM((4, CH - W, BLOCK), BF16),
                pltpu.VMEM((COUNT, 2, 8, PART, HALF), F32),
                pltpu.VMEM((COUNT, 8, PART, HALF), F32),
                pltpu.VMEM((COUNT, 2, 4, PART, HALF), F32),
                pltpu.VMEM((COUNT, PART, HALF), F32),
                pltpu.VMEM((2, 2, 2, PART, CH), F32),
                pltpu.VMEM((2, 2, 2, PART, CH), F32),
                pltpu.VMEM((2, 2, 2, 2, PART, CH), F32),
                pltpu.VMEM((2, 2, 2, PART, CH), F32),
                pltpu.VMEM((2, 14, 2, PART, 4 * ROWS), F32),
                pltpu.VMEM((3, 2, 8, PART, 4 * ROWS), F32),
                pltpu.VMEM((3, 8, 2, PART, 4 * ROWS), F32),
                pltpu.VMEM((2, 2, PART, CH), F32),
                pltpu.VMEM((8, PART, 4 * ROWS), F32),
                pltpu.VMEM((8, PART, 4 * ROWS), F32),
                dma((1,)), dma((12,)),
                dma((5,)), dma((4, 5)),
                dma((1,)), dma((COUNT,)),
                dma((1,)), dma((COUNT, 4)),
                dma((3,)), dma((3,)),
                dma((3,)), dma((4, 2)),
                dma((2,)), dma((4, 2)),
                dma((1,)),
            ],
            compiler_params=pltpu.CompilerParams(
                collective_id=0, has_side_effects=True, vmem_limit_bytes=56 * 1024 * 1024),
            cost_estimate=pl.CostEstimate(flops=14 * 10**9, bytes_accessed=3 * 2**20, transcendentals=0),
            name="gram",
        )(activations)

    return jax.shard_map(shards, mesh=mesh, in_specs=(P("tok", "col"),), out_specs=P(("col", "tok"), None), check_vma=False)
```

```python
import jax
import jax.numpy as jnp
from jax import lax
from jax.experimental import pallas as pl
from jax.experimental.pallas import tpu as pltpu
from jax.sharding import PartitionSpec as P

MESH = pl.DeviceIdType.MESH
F32, BF16 = jnp.float32, jnp.bfloat16
BLOCK = 1024
HALF = BLOCK // 2
CH = HALF // 2
ROWS = 32
PART = ROWS // 2
W = 80
LAST = (((1,), (1,)), ((), ()))
A, B = 0, 1
OWN, PEER, SELF, NEXT, FAR = range(5)
CELLS = (
    ((OWN, A, "p", A), (OWN, A, "p", B),),
    ((OWN, A, "r", A), (OWN, A, "r", B),),
    ((OWN, B, "p", A), (OWN, B, "p", B),),
    ((OWN, B, "r", A), (OWN, B, "r", B),),
    ((PEER, A, "p", A), (PEER, A, "p", B),),
    ((PEER, A, "r", A), (PEER, A, "r", B),),
    ((PEER, B, "p", A), (PEER, B, "p", B),),
    ((PEER, B, "r", A), (PEER, B, "r", B),),
    ((NEXT, A, "0", A), (SELF, B, "u", A),),
    ((NEXT, A, "r", B), (NEXT, B, "r", B),),
    ((FAR, A, "f", B), (NEXT, B, "0", B),),
    ((FAR, A, "g", B), (FAR, B, "g", B),),
    ((SELF, A, "u", B),),
    ((NEXT, A, "1", A),),
    ((NEXT, A, "p", A),),
    ((FAR, B, "f", B),),
    ((NEXT, B, "p", A),),
    ((NEXT, A, "p", B),),
    ((NEXT, B, "r", A), (FAR, B, "g", A),),
    ((NEXT, B, "p", B), (SELF, A, "u", A),),
    ((NEXT, B, "0", A), (SELF, B, "u", B),),
    ((FAR, B, "f", A),),
    ((NEXT, B, "1", B),),
    ((FAR, A, "g", A),),
    ((NEXT, A, "0", B),),
    ((NEXT, A, "1", B), (NEXT, B, "1", A),),
    ((FAR, A, "f", A),),
    ((NEXT, A, "r", A),),
)
COUNT = len(CELLS)
PAIRS = sum(len(tiles) for tiles in CELLS) // 2
X_NEEDS = {("p", A): (1,), ("p", B): (3,), ("r", A): (7,), ("r", B): (11,), ("0", A): (0, 4, 5), ("0", B): (2, 8, 9),
           ("1", A): (0, 4, 6), ("1", B): (2, 8, 10), ("f", A): (1, 0, 4, 5, 6), ("f", B): (3, 2, 8, 9, 10),
           ("g", A): (7, 0, 4, 5, 6), ("g", B): (11, 2, 8, 9, 10), ("u", A): (0, 4, 5, 6), ("u", B): (2, 8, 9, 10)}
X_FORWARD = {1: 0, 3: 2, 7: 4, 11: 8}
X_GROUPS = ((0, 2), (1, 5), (3, 4, 6, 8, 10, 9), (11,), (7,))
OWN_FIRST = True

ORDER = (
    ('c', 0), ('c', 1), ('c', 2), ('c', 3), ('c', 4), ('c', 5), ('c', 6), ('z', 0, 0),
    ('c', 7), ('z', 1, 0), ('z', 2, 0), ('x', 1), ('z', 3, 0), ('z', 4, 0), ('z', 5, 0), ('z', 6, 0),
    ('z', 0, 1), ('z', 7, 0), ('z', 1, 1), ('z', 2, 1), ('z', 3, 1), ('z', 4, 1), ('z', 5, 1), ('y', 0, 0, 4),
    ('z', 6, 1), ('z', 0, 2), ('z', 7, 1), ('x', 2), ('z', 1, 2), ('z', 2, 2), ('z', 3, 2), ('z', 4, 2),
    ('z', 5, 2), ('z', 6, 2), ('z', 0, 3), ('z', 7, 2), ('t', 0), ('y', 0, 1, 4), ('z', 1, 3), ('z', 2, 3),
    ('z', 3, 3), ('z', 4, 3), ('z', 5, 3), ('z', 6, 3), ('f', 0), ('z', 7, 3), ('f', 1), ('f', 2),
    ('f', 3), ('f', 4), ('f', 5), ('f', 6), ('f', 7), ('t', 1), ('y', 1, 0, 4), ('y', 0, 0, 3),
    ('y', 1, 0, 3), ('y', 0, 1, 3), ('c', 14), ('c', 17), ('z', 14, 0), ('z', 17, 0), ('c', 8), ('c', 13),
    ('z', 14, 1), ('z', 17, 1), ('z', 8, 0), ('z', 13, 0), ('z', 14, 2), ('z', 17, 2), ('y', 1, 1, 3), ('z', 8, 1),
    ('z', 13, 1), ('z', 14, 3), ('z', 17, 3), ('c', 16), ('c', 19), ('x', 3), ('x', 4), ('peer',),
    ('z', 8, 2), ('z', 13, 2), ('z', 16, 0), ('c', 22), ('z', 19, 0), ('c', 25), ('z', 8, 3), ('z', 13, 3),
    ('z', 16, 1), ('z', 22, 0), ('z', 19, 1), ('z', 25, 0), ('c', 26), ('y', 1, 1, 4), ('f', 14), ('f', 17),
    ('z', 16, 2), ('z', 22, 1), ('c', 10), ('z', 19, 2), ('c', 12), ('z', 25, 1), ('z', 26, 0), ('c', 20),
    ('c', 24), ('z', 16, 3), ('z', 22, 2), ('z', 10, 0), ('z', 12, 0), ('z', 19, 3), ('z', 25, 2), ('z', 20, 0),
    ('z', 26, 1), ('z', 24, 0), ('f', 8), ('c', 9), ('f', 13), ('z', 22, 3), ('f', 16), ('z', 10, 1),
    ('z', 12, 1), ('f', 19), ('z', 25, 3), ('z', 9, 0), ('z', 20, 1), ('z', 24, 1), ('z', 26, 2), ('c', 11),
    ('c', 15), ('z', 10, 2), ('z', 12, 2), ('c', 21), ('z', 20, 2), ('z', 9, 1), ('c', 18), ('z', 24, 2),
    ('z', 26, 3), ('z', 11, 0), ('c', 23), ('z', 15, 0), ('f', 22), ('c', 27), ('z', 21, 0), ('f', 25),
    ('z', 10, 3), ('z', 12, 3), ('z', 18, 0), ('z', 23, 0), ('z', 9, 2), ('z', 27, 0), ('z', 11, 1), ('z', 15, 1),
    ('z', 20, 3), ('z', 21, 1), ('z', 24, 3), ('f', 26), ('f', 10), ('own',), ('f', 12), ('z', 18, 1),
    ('z', 23, 1), ('z', 9, 3), ('z', 27, 1), ('z', 11, 2), ('z', 15, 2), ('f', 20), ('z', 21, 2), ('f', 24),
    ('z', 18, 2), ('z', 23, 2), ('f', 9), ('z', 27, 2), ('z', 11, 3), ('z', 15, 3), ('z', 21, 3), ('z', 18, 3),
    ('z', 23, 3), ('z', 27, 3), ('u',), ('m', 0, 0), ('m', 0, 1), ('f', 11), ('f', 15), ('f', 21),
    ('f', 18), ('m', 1, 1), ('f', 23), ('f', 27), ('m', 2, 1), ('m', 2, 0), ('m', 1, 0), ('next',),
    ('self',), ('far',),
)


def kernel(scale, given_ref, out_ref, a_ref, G, Q, QP, RL, T, CR, ZR, R, PR, D, O1, O2, MB, MT, MO, DU, MTU, MOU,
           xs, xr, ys, yr, cs, cr, zs, zr, ds, dr, ms, mr, ts, tr, os):
    col, tok = lax.axis_index("col"), lax.axis_index("tok")
    lo, y = col // 4, col % 4
    z, hi, c = tok // 4, (tok // 2) % 2, tok % 2
    x = 2 * hi + lo
    s = y // 2

    def at(x_, y_, z_, c_):
        return ((x_ % 2) * 4 + y_, z_ * 4 + (x_ // 2) * 2 + c_)

    x_next, x_prev, x_opposite = (x + 1) % 4, (x + 3) % 4, (x + 2) % 4
    y_next, y_prev, y_far = (y + 1) % 4, (y + 3) % 4, (y + 2) % 4
    x_dev = (at(x_next, y, z, c), at(x_prev, y, z, c))
    x_from = (x_prev, x_next)
    y_up, y_down = at(x, y_next, z, c), at(x, y_prev, z, c)
    sibling = at(x, y, z, 1 - c)
    z_dev = (at(x, y, (z + 1) % 8, c), at(x, y, (z + 7) % 8, c))
    far_lo = (lo + s) % 2
    half_lo = {"p": lo, "r": lo, "0": 1 - lo, "1": 1 - lo, "f": far_lo, "g": far_lo, "u": 1 - lo}
    half_h = {"p": hi, "r": 1 - hi, "0": 0, "1": 1, "f": hi, "g": 1 - hi, "u": x_next // 2}

    def send(src, dst, s_sem, r_sem, dev):
        cp = pltpu.make_async_remote_copy(src_ref=src, dst_ref=dst, send_sem=s_sem, recv_sem=r_sem,
                                          device_id=dev, device_id_type=MESH)
        cp.start()

    def taken(ref, sem):
        pltpu.make_async_copy(ref, ref, sem).wait()

    partners = [at(2 * (hi ^ dh) + (lo ^ dl), y, z, c ^ dc)
                for dh in range(2) for dl in range(2) for dc in range(2) if dh + dl + dc]
    partners += [at(x, y, (z + dz) % 8, c) for dz in range(1, 8)]
    partners += [at(x, (y + dy) % 4, z, c) for dy in range(1, 4)]
    barrier = pltpu.get_barrier_semaphore()
    for dev in partners:
        pl.semaphore_signal(barrier, inc=1, device_id=dev, device_id_type=MESH)
    given = pltpu.make_async_copy(given_ref, a_ref, os.at[0])
    given.start()

    def reorder(h, part):
        p = lax.broadcasted_iota(jnp.int32, (BLOCK, HALF), 1)
        f = lax.broadcasted_iota(jnp.int32, (BLOCK, HALF), 0)
        feature = ((p // PART) % 8) * 128 + h * 64 + ((p // 128) % 2) * 32 + (p // CH) * PART + p % PART
        pick = (f == feature).astype(F32).astype(BF16)
        rows = pl.ds(part * HALF, HALF)
        v = jnp.dot(a_ref[rows, :], pick, preferred_element_type=F32).astype(BF16)
        for cc in (A, B):
            G[x, h, cc, rows, :] = v[:, cc * CH:cc * CH + CH]

    def turn(x_, h, cc, dst):
        r = lax.broadcasted_iota(jnp.int32, (CH, CH), 0)
        f = lax.broadcasted_iota(jnp.int32, (CH, CH), 1)
        one = (r == f).astype(F32).astype(BF16)
        dst[...] = lax.dot_general(one, G[x_, h, cc], LAST, preferred_element_type=F32).astype(BF16)

    def h_of(x_):
        return x_ // 2

    def x_sent(n, d):
        b = x_from[d]
        return {0: (x, 1 - hi, A, d), 1: (b, 1 - h_of(b), A, d), 2: (x, 1 - hi, B, d), 3: (b, 1 - h_of(b), B, d),
                4: (x, hi, A, d), 5: (x, 0, A, 1 - d), 6: (x, 1, A, 1 - d), 7: (b, h_of(b), A, d),
                8: (x, hi, B, d), 9: (x, 0, B, 1 - d), 10: (x, 1, B, 1 - d), 11: (b, h_of(b), B, d)}[n]

    def x_unit(x_, h, cc, part):
        return G.at[x_, h, cc, pl.ds(part * HALF, HALF), :]

    def x_send(*messages):
        for n in messages:
            for d in range(2):
                u = x_unit(*x_sent(n, d))
                send(u, u, xs.at[0], xr.at[n], x_dev[d])

    low, high = pl.ds(0, W), pl.ds(W, CH - W)
    slots = (hi, 1 - hi)

    def y_landing(k, r, m):
        q = slots[k]
        return (Q.at[1, q, r, low], Q.at[1, q, r, high], RL.at[2 * k + r], Q.at[2, q, r, low], Q.at[2, q, r, high])[m]

    def y_send(k, r, *messages):
        for m in messages:
            q = slots[k]
            src = (Q.at[0, q, r, low], Q.at[0, q, r, high], Q.at[0, q, r, high], Q.at[1, q, r, low], RL.at[2 * k + r])[m]
            send(src, y_landing(k, r, m), ys.at[m], yr.at[2 * k + r, m], y_down if m in (0, 1, 3) else y_up)

    waited = set()

    def need_x(*messages):
        for n in messages:
            if ("x", n) not in waited:
                waited.add(("x", n))
                taken(G.at[0, 0, 0], xr.at[n])

    def need_y(k, r, *messages):
        for m in messages:
            if ("y", k, r, m) not in waited:
                waited.add(("y", k, r, m))
                taken(y_landing(k, r, m), yr.at[2 * k + r, m])

    def x_step(n):
        if n:
            need_x(X_FORWARD[X_GROUPS[n][0]])
        x_send(*X_GROUPS[n])

    def q_step(r):
        need_x((1, 3)[r])
        turn(x_opposite, hi, r, Q.at[0, 1 - hi, r])
        y_send(1, r, 0, 2, 1)
        if r == A and not OWN_FIRST:
            y_send(0, B, 0, 2, 1)

    def y_step(k, r, m):
        need_y(k, r, 0 if m == 3 else 2)
        y_send(k, r, m)

    def compute(cell):
        for j, (kind, r, half, cc) in enumerate(CELLS[cell]):
            l, h = half_lo[half], half_h[half]
            if kind in (OWN, PEER):
                rows = QP[r] if kind == PEER else Q[0, hi, r]
                acc = jnp.dot(rows, G[x, h, cc], preferred_element_type=F32)
            else:
                need_x(*X_NEEDS[half, cc])
                for k in range(2):
                    need_y(k, r, *((), (0, 1), (3, 4))[kind - SELF])
                acc = jnp.dot(Q[kind - SELF, 0, r], G[l, h, cc], preferred_element_type=F32)
                acc += jnp.dot(Q[kind - SELF, 1, r], G[2 + l, h, cc], preferred_element_type=F32)
            T[cell, :, :, :, j * CH:j * CH + CH] = acc.reshape(2, 8, PART, CH)
        w = width(cell)
        send(T.at[cell, 1 - c, :, :, w], CR.at[cell, :, :, w], cs.at[0], cr.at[cell], sibling)

    def width(cell):
        return pl.ds(0, CH * len(CELLS[cell]))

    def z_landed(cell, step):
        w = width(cell)
        taken(ZR.at[cell, :, step, :, w] if step else ZR.at[cell, 0, 0, :, w], zr.at[cell, step])

    def z_step(cell, step):
        w, n = width(cell), CH * len(CELLS[cell]) // 2
        sides = (pl.ds(0, n), pl.ds(n, n))
        if step == 0:
            taken(CR.at[cell, :, :, w], cr.at[cell])
        else:
            z_landed(cell, step - 1)
        for d in range(2):
            to = (z + 4 - step) % 8 if d == 0 else (z + 4 + step) % 8
            if step == 0:
                cols = sides[d]
                T[cell, c, to, :, cols] = T[cell, c, to, :, cols] + CR[cell, to, :, cols]
                send(T.at[cell, c, to, :, cols], ZR.at[cell, d, 0, :, cols], zs.at[0], zr.at[cell, 0], z_dev[d])
                continue
            if step == 1:
                cols, rest = sides[d], sides[1 - d]
                T[cell, c, to, :, cols] = T[cell, c, to, :, cols] + CR[cell, to, :, cols] + ZR[cell, d, 0, :, cols]
                T[cell, c, to, :, rest] = T[cell, c, to, :, rest] + CR[cell, to, :, rest]
            else:
                T[cell, c, to, :, w] = T[cell, c, to, :, w] + CR[cell, to, :, w] + ZR[cell, d, step - 1, :, w]
            send(T.at[cell, c, to, :, w], ZR.at[cell, d, step, :, w], zs.at[0], zr.at[cell, step], z_dev[d])

    def out_cols(l, y_):
        return pl.ds(pl.multiple_of((l * 4 + y_) * BLOCK, BLOCK), BLOCK)

    def group(j, k):
        return pl.ds(pl.multiple_of(j * CH + k * 128, 128), 128)

    def mirror_self(half, k):
        return "no" if k else {"p": "yes", "f": "some"}.get(half, "no")

    def finish(cell):
        z_landed(cell, 3)
        w = width(cell)
        R[cell, :, w] = T[cell, c, z, :, w] + CR[cell, z, :, w] + ZR[cell, 0, 3, :, w] + ZR[cell, 1, 3, :, w]
        for j, (kind, r, half, cc) in enumerate(CELLS[cell]):
            l, h = half_lo[half], half_h[half]
            cols = pl.ds(j * CH, CH)
            src = R.at[cell, :, cols]
            if kind == OWN:
                D[h, cc, r] = R[cell, :, cols]
                continue
            if kind == SELF:
                DU[cc, r] = R[cell, :, cols]
                for k in range(2):
                    send(R.at[cell, :, pl.ds(j * CH + k * 128, 128)], MB.at[cc, 12 + c, r], ms.at[2], mr.at[3, 0],
                         at(x_next, y, z, k))
                continue
            if kind == PEER:
                continue
            mine = (8 if kind == FAR else lo * 4) + hi * 2 + c
            s_sem, batch = ms.at[kind - NEXT], 2 if kind == FAR else 1 if half in "pr" else 0
            for dk in range(2):
                k = (c + dk) % 2
                part, dst, dev = R.at[cell, :, group(j, k)], MB.at[cc, mine, r], at(2 * h + l, y, z, k)
                stays = mirror_self(half, dk)

                def leave():
                    send(part, dst, s_sem, mr.at[batch, cc], dev)

                def keep():
                    MB[cc, mine, r] = R[cell, :, group(j, k)]
                if stays == "no":
                    leave()
                elif stays == "yes":
                    keep()
                else:
                    pl.when(s == 0)(keep)
                    pl.when(s == 1)(leave)
            if kind == NEXT:
                send(src, O1.at[l, h, cc, r], ds.at[1], dr.at[1], y_up)
            else:
                send(src, O2.at[h, cc, r], ds.at[2], dr.at[2], at(x, y_far, z, c))

    def send_peer():
        for cell, tiles in enumerate(CELLS):
            for j, (kind, r, half, cc) in enumerate(tiles):
                if kind == PEER:
                    send(R.at[cell, :, pl.ds(j * CH, CH)], PR.at[half_h[half], cc, r], ds.at[0], dr.at[0], at(x_opposite, y, z, c))

    mirror_base = ((1 - lo) * 4, lo * 4, 8)

    def mirror(b, cc):
        def take(n):
            taken(MB.at[cc, 0:n], mr.at[b, cc])
        if b < 2:
            take(4 - b)
        else:
            pl.when(s == 0)(lambda: take(3))
            pl.when(s == 1)(lambda: take(4))
        turned = jnp.transpose(MB[cc, pl.ds(mirror_base[b], 4)].reshape(4 * ROWS, 4 * ROWS))
        MT[b, cc] = turned.reshape(8, PART, 4 * ROWS) * scale
        MO[b, z, cc] = MT[b, cc, z]
        for dz in range(1, 8):
            to = (z + dz) % 8
            send(MT.at[b, cc, to], MO.at[b, z, cc], ts.at[0], tr.at[b, cc], at(x, y, to, c))

    def mirror_next_x():
        taken(MB.at[0, 0:4], mr.at[3, 0])
        turned = [jnp.transpose(MB[cc, 12:14].reshape(2 * ROWS, 4 * ROWS)).reshape(8, PART, 2 * ROWS) for cc in (A, B)]
        MTU[...] = jnp.concatenate(turned, axis=2) * scale
        MOU[z] = MTU[z]
        for dz in range(1, 8):
            to = (z + dz) % 8
            send(MTU.at[to], MOU.at[z], ts.at[1], tr.at[3, 0], at(x, y, to, c))

    def store(l, y_, v):
        out_ref[:, out_cols(l, y_)] = v

    def natural(v):
        t = [[v[h, cc].reshape(ROWS, CH) for cc in (A, B)] for h in range(2)]
        return scale * jnp.concatenate([t[h][cc][:, k * 128 + b * PART:k * 128 + b * PART + PART]
                                        for b in range(8) for h in range(2) for k in range(2) for cc in (A, B)], axis=1)

    def store_mirror(b, l, y_):
        for cc in (A, B):
            taken(MO.at[b, 0:7, cc], tr.at[b, cc])
        store(l, y_, jnp.concatenate([MO[b, k].reshape(ROWS, 4 * ROWS) for k in range(8)], axis=1))

    def store_own():
        taken(PR, dr.at[0])
        store(lo, y, natural(D[...] + PR[...]))

    def store_next():
        taken(O1, dr.at[1])
        for l in range(2):
            store(l, y_prev, natural(O1[l]))

    def store_far():
        taken(O2, dr.at[2])
        store((lo + 1 - s) % 2, y_far, natural(O2[...]))

    def store_self():
        taken(MOU.at[0:7], tr.at[3, 0])
        direct = [DU[cc].reshape(ROWS, CH) * scale for cc in (A, B)]
        first = x_next // 2 == 0
        groups = []
        for b in range(8):
            own = jnp.concatenate([direct[cc][:, k * 128 + b * PART:k * 128 + b * PART + PART]
                                   for k in range(2) for cc in (A, B)], axis=1)
            other = jnp.concatenate([MOU[b, :, cc * 64:cc * 64 + 64] for cc in (A, B)], axis=0)
            groups += [jnp.where(first, own, other), jnp.where(first, other, own)]
        store(1 - lo, y, jnp.concatenate(groups, axis=1))

    given.wait()
    for part in range(2):
        reorder(1 - hi, part)
    pl.semaphore_wait(barrier, len(partners))
    x_step(0)
    for part in range(2):
        reorder(hi, part)
    turn(x, hi, A, Q.at[0, hi, A])
    y_send(0, A, 0, 2, 1)
    turn(x, hi, B, Q.at[0, hi, B])
    if OWN_FIRST:
        y_send(0, B, 0, 2, 1)
    for cc in (A, B):
        turn(x, 1 - hi, cc, QP.at[cc])

    steps = {"x": x_step, "t": q_step, "u": mirror_next_x, "y": y_step, "c": compute, "z": z_step, "f": finish, "m": mirror, "peer": send_peer, "own": store_own, "next": store_next,
             "far": store_far, "self": store_self}
    for name, *which in ORDER:
        steps[name](*which)
    store_mirror(0, 1 - lo, y_next)
    store_mirror(1, lo, y_next)
    store_mirror(2, far_lo, y_far)

    taken(G.at[0:3], xs.at[0])
    for m in range(5):
        taken(Q.at[0, :, :, low if m in (0, 3) else high], ys.at[m])
    taken(CR.at[0:PAIRS], cs.at[0])
    taken(CR.at[0:PAIRS, 0:7], zs.at[0])
    for n, ref in enumerate((PR, O1, O2)):
        taken(ref, ds.at[n])
    taken(MB.at[:, 0:7], ms.at[0])
    for v in range(2):
        pl.when(s == v)(lambda: taken(MB.at[:, 0:3 + v], ms.at[1]))
    taken(MB.at[0, 0:4], ms.at[2])
    taken(MT.at[:, :, 0:7], ts.at[0])
    taken(MTU.at[0:7], ts.at[1])


def solution(mesh):
    token_ranks = mesh.shape["tok"]

    def shards(activations):
        scale = 1.0 / (activations.shape[0] * token_ranks)
        dma = pltpu.SemaphoreType.DMA
        return pl.pallas_call(
            lambda *refs: kernel(scale, *refs),
            out_shape=pltpu.VMEM((ROWS, 8 * BLOCK), F32),
            in_specs=[pl.BlockSpec(memory_space=pl.ANY)],
            out_specs=pl.BlockSpec(memory_space=pltpu.VMEM),
            scratch_shapes=[
                pltpu.VMEM((BLOCK, BLOCK), BF16),
                pltpu.VMEM((4, 2, 2, BLOCK, CH), BF16),
                pltpu.VMEM((3, 2, 2, CH, BLOCK), BF16),
                pltpu.VMEM((2, CH, BLOCK), BF16),
                pltpu.VMEM((4, CH - W, BLOCK), BF16),
                pltpu.VMEM((COUNT, 2, 8, PART, HALF), F32),
                pltpu.VMEM((COUNT, 8, PART, HALF), F32),
                pltpu.VMEM((COUNT, 2, 4, PART, HALF), F32),
                pltpu.VMEM((COUNT, PART, HALF), F32),
                pltpu.VMEM((2, 2, 2, PART, CH), F32),
                pltpu.VMEM((2, 2, 2, PART, CH), F32),
                pltpu.VMEM((2, 2, 2, 2, PART, CH), F32),
                pltpu.VMEM((2, 2, 2, PART, CH), F32),
                pltpu.VMEM((2, 14, 2, PART, 4 * ROWS), F32),
                pltpu.VMEM((3, 2, 8, PART, 4 * ROWS), F32),
                pltpu.VMEM((3, 8, 2, PART, 4 * ROWS), F32),
                pltpu.VMEM((2, 2, PART, CH), F32),
                pltpu.VMEM((8, PART, 4 * ROWS), F32),
                pltpu.VMEM((8, PART, 4 * ROWS), F32),
                dma((1,)), dma((12,)),
                dma((5,)), dma((4, 5)),
                dma((1,)), dma((COUNT,)),
                dma((1,)), dma((COUNT, 4)),
                dma((3,)), dma((3,)),
                dma((3,)), dma((4, 2)),
                dma((2,)), dma((4, 2)),
                dma((1,)),
            ],
            compiler_params=pltpu.CompilerParams(
                collective_id=0, has_side_effects=True, vmem_limit_bytes=56 * 1024 * 1024),
            cost_estimate=pl.CostEstimate(flops=14 * 10**9, bytes_accessed=3 * 2**20, transcendentals=0),
            name="gram",
        )(activations)

    return jax.shard_map(shards, mesh=mesh, in_specs=(P("tok", "col"),), out_specs=P(("col", "tok"), None), check_vma=False)
```
